32 devices in a mesh: pix: 8 (over z, y), chan: 4 (over x, core).
Axes of the slice: x: 2, y: 2, z: 4, core: 2. Of those that a mesh axis runs over, the one named last changes fastest.
Arguments:
- spectra: bfloat16 [32768, 2048], P('pix', 'chan'), may hold values from 0.05 to 2100, as said below
- start: bfloat16 [64, 2048], P(None, 'chan'), may hold values from -6 to 6
- anchors: int32 [16], replicated, may hold values from 0 to 32767, as said below
Outputs:
- scores: float32 [64, 32768], P(None, 'pix')
- abundance: float32 [16, 32768], P(None, 'pix')
The draws below stay inside these ranges and needn't reach their ends.
Inputs may be any that keep to these rules, and one draw needn't show every extreme that they name: `spectra`: every entry is positive. `anchors`: the 16 indices are distinct; pixel 0 and pixel 32768 - 1 are among them.
All inputs are finite; a program needn't handle non-finite values.
Results may differ from the reference program's by a relative error of at most 0.035.
Values may be sent and summed in bfloat16 or wider, within the bound.
A program may use at most 64 MiB of HBM per device.

```python
import math
import jax
import jax.numpy as jnp
from jax import lax

CH = 2048
K = 64
NA = 16
ITERS = 5
PIX_DEV = 4096
PIX = 32768
N_PIX = 8
N_CHAN = 4


def draw_spectra(key, part):
    key_row, key_col, key_unit = jax.random.split(jax.random.fold_in(key, 11), 3)
    place = jnp.arange(PIX, dtype=jnp.float32) / max(PIX - 1, 1)
    energy = jnp.arange(CH, dtype=jnp.float32) / max(CH - 1, 1) - 0.5
    rise_pix = jnp.exp(math.log(3.0) * place)
    col_scale = jnp.exp(jax.random.uniform(key_col, (CH,), jnp.float32) * math.log(10.0))
    row_scale = jnp.exp(jax.random.uniform(key_row, (PIX,), jnp.float32) * math.log(10.0)) * rise_pix
    unit = jax.random.uniform(key_unit, (PIX, CH), jnp.float32, 0.25, 1.75)
    slope = math.log(8.0)
    tilt = jnp.exp(slope * place[:, None] * energy[None, :])
    values = unit * row_scale[:, None] * col_scale[None, :] * tilt
    return values.astype(jnp.bfloat16)


def draw_anchors(key, part):
    order = jax.random.permutation(jax.random.fold_in(key, 7), PIX - 2) + 1
    inner = order[:NA - 2].astype(jnp.int32)
    ends = jnp.array([0, PIX - 1], dtype=jnp.int32)
    return jnp.concatenate([ends[:1], inner, ends[1:]]).astype(jnp.int32)


def levels(stream_key, extent, cuts, least, high):
    loudness = 1.0
    for dim, blocks in cuts:
        draws = jax.random.uniform(jax.random.fold_in(jax.random.fold_in(stream_key, 6), dim), (blocks,), jnp.float32, least / len(cuts), high / len(cuts))
        loudness = loudness * jnp.repeat(jnp.exp(draws), extent[dim] // blocks).reshape((-1,) + (1,) * (len(extent) - 1 - dim))
    return loudness


def bell_draw(own_key, extent, deviation, limit, cuts=(), kind=jnp.bfloat16):
    drawn = deviation * jax.random.normal(own_key, extent, jnp.float32)
    if cuts:
        drawn = drawn * levels(own_key, extent, cuts, -0.22, 0.18)
    return jnp.clip(drawn, -limit, limit).astype(kind)


def setup_inputs(seed: int = 0) -> dict:
    splits = jax.random.split(jax.random.key(seed), 4)
    return {
        "spectra": draw_spectra(jax.random.fold_in(splits[3], 71), 0),
        "start": bell_draw(splits[1], (K, CH), 1.0, 6.0, ((1, 4),)),
        "anchors": draw_anchors(jax.random.fold_in(splits[3], 71), 0),
    }


def weigh(block, rowsum, colsum, total):
    expect = rowsum[:, None] * colsum[None, :] / total
    return ((block.astype(jnp.float32) - expect) * lax.rsqrt(expect)).astype(jnp.bfloat16)

def tri_solve(lower, rhs):
    return lax.linalg.triangular_solve(lower, rhs, left_side=True, lower=True)

def reference(spectra, start, anchors):
    rowsum = lax.optimization_barrier(jnp.sum(spectra, axis=1, dtype=jnp.float32))
    colsum = lax.optimization_barrier(jnp.sum(spectra, axis=0, dtype=jnp.float32))
    total = jnp.sum(colsum)
    blocks = spectra.reshape(N_PIX, PIX_DEV, CH)
    row_blocks = rowsum.reshape(N_PIX, PIX_DEV)
    group = CH // N_CHAN
    loadings = start
    for step in range(ITERS):

        def visit(acc, item):
            block, rows_here = item
            weighted = weigh(block, rows_here, colsum, total)
            summed = jnp.zeros((K, PIX_DEV), jnp.float32)
            for g in range(N_CHAN):
                part = jnp.dot(loadings[:, g * group:(g + 1) * group].astype(jnp.float32), weighted[:, g * group:(g + 1) * group].T.astype(jnp.float32), preferred_element_type=jnp.float32)
                summed = summed + part.astype(jnp.bfloat16).astype(jnp.float32)
            proj = summed.astype(jnp.bfloat16)
            return (acc + jnp.dot(proj.astype(jnp.float32), weighted.astype(jnp.float32), preferred_element_type=jnp.float32), None)
        back, unused = lax.scan(visit, jnp.zeros((K, CH), jnp.float32), (blocks, row_blocks))
        gram = jnp.dot(back, back.T, precision=lax.Precision.HIGHEST)
        lower = jnp.linalg.cholesky(gram)
        loadings = tri_solve(lower, back).astype(jnp.bfloat16)

    def score_block(item):
        block, rows_here = item
        weighted = weigh(block, rows_here, colsum, total)
        return jnp.dot(loadings.astype(jnp.float32), weighted.T.astype(jnp.float32), preferred_element_type=jnp.float32)
    scores = lax.map(score_block, (blocks, row_blocks))
    scores = jnp.transpose(scores, (1, 0, 2)).reshape(K, PIX)
    rows = scores[:, anchors.astype(jnp.int32)].T
    small = jnp.dot(rows, rows.T, precision=lax.Precision.HIGHEST)
    lower = jnp.linalg.cholesky(small)
    rhs = jnp.dot(rows, scores, precision=lax.Precision.HIGHEST)
    middle = tri_solve(lower, rhs)
    abundance = lax.linalg.triangular_solve(lower, middle, left_side=True, lower=True, transpose_a=True)
    return (scores, abundance)
```

```python
import functools

import jax
import jax.numpy as jnp
from jax import lax
from jax.experimental import pallas as pl
from jax.experimental.pallas import tpu as pltpu
from jax.sharding import PartitionSpec as P

ITERS = 5
GROUP = 8
MESH = pl.DeviceIdType.MESH
HIGH = lax.Precision.HIGHEST
F32 = jnp.float32
BF16 = jnp.bfloat16
NT = (((1,), (1,)), ((), ()))


def dot(a, b, dims=(((1,), (0,)), ((), ())), precision=None):
    return lax.dot_general(a, b, dims, precision=precision, preferred_element_type=F32)


def inverse_factor(gram):
    n = gram.shape[0]
    rows = lax.broadcasted_iota(jnp.int32, (n, 128), 0)
    lanes = lax.broadcasted_iota(jnp.int32, (n, 128), 1)
    full = jnp.where(lanes == rows, 1.0, gram)
    sub = lax.broadcasted_iota(jnp.int32, (8, 128), 0)
    blocks = [full[8 * i : 8 * i + 8, :] for i in range(n // 8)]
    for k in range(n):
        home, r = k // 8, k % 8
        row = blocks[home][r : r + 1, :]
        scaled = row * (1.0 / row[:, 64 + k : 65 + k])
        for i in range(home, n // 8):
            column = blocks[i][:, 64 + k : 65 + k]
            change = column * scaled
            if i == home:
                change = jnp.where(sub > r, change, 0.0)
            blocks[i] = blocks[i] - change
    full = jnp.concatenate(blocks, axis=0)
    pivots = jnp.sum(jnp.where(lanes == rows + 64, full, 0.0), axis=1, keepdims=True)
    return jnp.where(lanes < 64, full * lax.rsqrt(pivots), 0.0)


def kernel(
    n_pix, s_ref, start_ref, anchors_ref, scores_ref, abund_ref,
    other_s, start_in, col_out, col_in, col_mine, col_chan, row_out, row_in, row_sum,
    w, wt, load, x_out, x_in, acc, half_in, keep, rs_in, hi_in, ag, back_in, padded,
    gram_out, gram_in, score, rows_half, rows_half_in, rows_out, rows_in, rows_pad,
    s_sem, st_sem, col_sem, cc_sem, row_sem, x_sem, half_sem, rs_sem, hi_sem, ag_sem,
    bk_sem, gram_sem, sc_sem, rh_sem, rows_sem,
):
    pix = lax.axis_index("pix")
    chan = lax.axis_index("chan")
    lo, hi = lax.rem(chan, 2), lax.div(chan, 2)
    mates = [hi * 2 + 1 - lo, (1 - hi) * 2 + lo, (1 - hi) * 2 + 1 - lo]
    low = lax.rem(pix, GROUP)
    base = pix - low
    n_hi = n_pix // GROUP
    k_rows, ch = start_ref.shape
    pixels = s_ref.shape[0]
    half = pixels // 2
    step_pix = x_out.shape[-1]
    chunks = half // step_pix

    def send(src, dst, sems, device):
        return pltpu.make_async_remote_copy(
            src_ref=src, dst_ref=dst, send_sem=sems.at[0], recv_sem=sems.at[1],
            device_id=device, device_id_type=MESH,
        )

    def all_pix(f):
        def body(d, carry):
            f(d, lax.rem(pix + d, n_pix))
            return carry
        lax.fori_loop(1, n_pix, body, 0)

    barrier = pltpu.get_barrier_semaphore()
    for mate in mates:
        pl.semaphore_signal(barrier, inc=1, device_id=(pix, mate), device_id_type=MESH)
    all_pix(lambda d, to: pl.semaphore_signal(
        barrier, inc=1, device_id=(to, chan), device_id_type=MESH))
    pl.semaphore_wait(barrier, 3 + n_pix - 1)

    away = pl.multiple_of((1 - lo) * half, half)
    swap = send(s_ref.at[pl.ds(away, half)], other_s, s_sem, (pix, mates[0]))
    swap.start()
    swap_start = send(start_ref, start_in, st_sem, (pix, mates[0]))
    swap_start.start()

    ones = jnp.ones((8, step_pix), BF16)
    total_col = jnp.zeros((8, ch), F32)
    for j in range(2 * chunks):
        total_col += dot(ones, s_ref[j * step_pix : (j + 1) * step_pix, :])
    col_out[...] = total_col

    def col_copy(d, to):
        return send(col_out, col_in.at[d], col_sem.at[d], (to, chan))
    all_pix(lambda d, to: col_copy(d, to).start())

    ones_ch = jnp.ones((8, ch), BF16)
    for j in range(2 * chunks):
        sums = dot(ones_ch, s_ref[j * step_pix : (j + 1) * step_pix, :], NT)
        row_out[j : j + 1, :] = sums[0:1, :]
    row_copies = [
        send(row_out, row_in.at[m], row_sem.at[m], (pix, mates[m])) for m in range(3)
    ]
    for copy in row_copies:
        copy.start()

    col_in[0] = col_out[...]
    all_pix(lambda d, to: col_copy(d, to).wait())
    col_mine[...] = jnp.sum(col_in[...], axis=0)
    col_copies = [
        send(col_mine, col_chan.at[m], cc_sem.at[m], (pix, mates[m])) for m in range(3)
    ]
    for copy in col_copies:
        copy.start()
    for copy in row_copies:
        copy.wait()
    sums = (row_out[...] + row_in[0]) + (row_in[1] + row_in[2])
    for j in range(2 * chunks):
        row_sum[j] = jnp.broadcast_to(sums[j : j + 1, :], (8, step_pix))
    for copy in col_copies:
        copy.wait()
    cols = (col_mine[0:1, :] + col_chan[0, 0:1, :]) + (
        col_chan[1, 0:1, :] + col_chan[2, 0:1, :])
    inv_total = 1.0 / jnp.sum(cols, axis=1, keepdims=True)
    shares = [col_mine[0:1, :] * inv_total, col_chan[0, 0:1, :] * inv_total]
    swap.wait()

    tiles = step_pix // 128

    def weigh(i, carry):
        j, q = lax.div(i, tiles), lax.rem(i, tiles)
        first = pl.multiple_of(q * 128, 128)
        line = row_sum[lo * chunks + j, 0:1, pl.ds(first, 128)]
        wide = jnp.transpose(jnp.broadcast_to(line, (128, 128)))
        mine = s_ref[pl.ds(pl.multiple_of(lo * half + i * 128, 128), 128), :]
        theirs = other_s[pl.ds(pl.multiple_of(i * 128, 128), 128), :]
        for side, counts in enumerate((mine, theirs)):
            for g in range(ch // 128):
                expect = wide * shares[side][:, g * 128 : (g + 1) * 128]
                value = counts[:, g * 128 : (g + 1) * 128].astype(F32)
                weighted = (value - expect) * lax.rsqrt(expect)
                at = side * ch + g * 128
                w[j, pl.ds(first, 128), at : at + 128] = weighted.astype(BF16)
                wt[j, at : at + 128, pl.ds(first, 128)] = jnp.transpose(weighted).astype(BF16)
        return carry
    lax.fori_loop(0, chunks * tiles, weigh, 0)

    swap_start.wait()
    load[:, :ch] = start_ref[...]
    load[:, ch:] = start_in[...]
    padded[...] = jnp.zeros_like(padded)
    rows_pad[...] = jnp.zeros_like(rows_pad)

    def x_copy(t, j):
        return send(x_out.at[t, j], x_in.at[t, j], x_sem.at[t, j], (pix, mates[1]))

    def project(t):
        def body(j, carry):
            x_out[t, j] = dot(load[...], wt[j]).astype(BF16)
            x_copy(t, j).start()
            return carry
        lax.fori_loop(0, chunks, body, 0)

    def gather(t, j):
        x_copy(t, j).wait()
        return x_out[t, j].astype(F32) + x_in[t, j].astype(F32)

    per = k_rows // GROUP

    def iteration(t, carry):
        project(t)
        acc[...] = jnp.zeros_like(acc)

        def body(j, carry):
            acc[...] += dot(gather(t, j).astype(BF16), w[j])
            return carry
        lax.fori_loop(0, chunks, body, 0)

        keep[t, 0] = acc[:, ch:]
        copy = send(keep.at[t, 0], half_in.at[t], half_sem.at[t], (pix, mates[0]))
        copy.start()
        copy.wait()
        keep[t, 1] = acc[:, :ch] + half_in[t]

        def partner(d):
            return lax.rem(low + d, GROUP)
        spread = [
            send(
                keep.at[t, 1, pl.ds(pl.multiple_of(partner(d) * per, per), per)],
                rs_in.at[t, d], rs_sem.at[t, d], (base + partner(d), chan))
            for d in range(1, GROUP)
        ]
        for copy in spread:
            copy.start()
        slab = keep[t, 1, pl.ds(pl.multiple_of(low * per, per), per), :]
        for d, copy in enumerate(spread, 1):
            copy.wait()
            slab = slab + rs_in[t, d]
        if n_hi > 1:
            hi_in[t, 0] = slab
            across = [
                send(hi_in.at[t, 0], hi_in.at[t, e], hi_sem.at[t, e],
                     (lax.rem(pix + e * GROUP, n_pix), chan))
                for e in range(1, n_hi)
            ]
            for copy in across:
                copy.start()
            for copy in across:
                copy.wait()
            slab = hi_in[t, lax.rem(n_hi + lax.div(pix, GROUP), n_hi)]
            for e in range(1, n_hi):
                slab = slab + hi_in[t, lax.rem(n_hi + lax.div(pix, GROUP) - e, n_hi)]
        mine = pl.ds(pl.multiple_of(low * per, per), per)
        ag[t, mine] = slab
        collect = [
            send(ag.at[t, mine], ag.at[t, mine], ag_sem.at[t, d], (base + partner(d), chan))
            for d in range(1, GROUP)
        ]
        for copy in collect:
            copy.start()
        for copy in collect:
            copy.wait()
        twin = send(ag.at[t], back_in.at[t], bk_sem.at[t], (pix, mates[0]))
        twin.start()
        back = ag[t]
        padded[k_rows : 2 * k_rows, :ch] = back
        gram_out[t] = dot(back, padded[: 2 * k_rows, :ch], NT, HIGH)
        grams = [
            send(gram_out.at[t], gram_in.at[t, m], gram_sem.at[t, m], (pix, mates[m]))
            for m in range(3)
        ]
        for copy in grams:
            copy.start()
        for copy in grams:
            copy.wait()
        gram = (gram_out[t] + gram_in[t, 0]) + (gram_in[t, 1] + gram_in[t, 2])
        factor = inverse_factor(gram)
        twin.wait()
        padded[k_rows : 2 * k_rows, ch:] = back_in[t]
        load[...] = dot(factor, padded[k_rows:, :], precision=HIGH).astype(BF16)
        return carry
    lax.fori_loop(0, ITERS, iteration, 0)

    project(ITERS)
    n_anchor = anchors_ref.shape[0]
    wanted = anchors_ref[...][:, :1] - pix * pixels - lo * half
    rows_half[...] = jnp.zeros_like(rows_half)

    def finish(j, carry):
        value = gather(ITERS, j)
        slot = lo * chunks + j
        score[slot] = value
        send(score.at[slot], score.at[slot], sc_sem.at[j], (pix, mates[0])).start()
        positions = lax.broadcasted_iota(jnp.int32, (n_anchor, step_pix), 1)
        picks = jnp.where(positions == wanted - j * step_pix, 1.0, 0.0)
        rows_half[...] += dot(picks, value, NT, HIGH)
        return carry
    lax.fori_loop(0, chunks, finish, 0)
    pair_rows = send(rows_half, rows_half_in, rh_sem, (pix, mates[0]))
    pair_rows.start()
    pair_rows.wait()
    rows_out[...] = rows_half[...] + rows_half_in[...]

    def rows_copy(d, to):
        return send(rows_out, rows_in.at[d], rows_sem.at[d], (to, chan))
    all_pix(lambda d, to: rows_copy(d, to).start())
    rows_in[0] = rows_out[...]
    for j in range(chunks):
        slot = lo * chunks + j
        send(score.at[slot], score.at[slot], sc_sem.at[j], (pix, mates[0])).wait()
    for j in range(2 * chunks):
        scores_ref[:, j * step_pix : (j + 1) * step_pix] = score[j]
    all_pix(lambda d, to: rows_copy(d, to).wait())
    rows = jnp.sum(rows_in[...], axis=0)
    rows_pad[64 : 64 + n_anchor, :] = rows
    small = dot(rows, rows_pad[0:128, :], NT, HIGH)
    factor = inverse_factor(small)
    solved = dot(factor, rows_pad[64:192, :], precision=HIGH)
    both = dot(jnp.transpose(factor)[:n_anchor, :], solved, precision=HIGH)
    for j in range(2 * chunks):
        abund_ref[:, j * step_pix : (j + 1) * step_pix] = dot(both, score[j], precision=HIGH)


def local(n_pix, spectra, start, anchors):
    pixels, ch = spectra.shape
    k = start.shape[0]
    na = anchors.shape[0]
    half = pixels // 2
    step = min(512, half)
    chunks = half // step
    n_hi = n_pix // GROUP
    spread = jnp.broadcast_to(anchors[:, None], (na, 128))
    vmem = pl.BlockSpec(memory_space=pltpu.VMEM)
    v = pltpu.VMEM
    sem = lambda *shape: pltpu.SemaphoreType.DMA(tuple(shape) + (2,))
    scratch = [
        v((half, ch), BF16), v((k, ch), BF16), v((8, ch), F32), v((n_pix, 8, ch), F32),
        v((8, ch), F32), v((3, 8, ch), F32), v((2 * chunks, step), F32),
        v((3, 2 * chunks, step), F32), v((2 * chunks, 8, step), F32),
        v((chunks, step, 2 * ch), BF16), v((chunks, 2 * ch, step), BF16), v((k, 2 * ch), BF16),
        v((ITERS + 1, chunks, k, step), BF16), v((ITERS + 1, chunks, k, step), BF16),
        v((k, 2 * ch), F32), v((ITERS, k, ch), F32), v((ITERS, 2, k, ch), F32),
        v((ITERS, GROUP, k // GROUP, ch), F32), v((ITERS, n_hi, k // GROUP, ch), F32),
        v((ITERS, k, ch), F32), v((ITERS, k, ch), F32), v((3 * k, 2 * ch), F32),
        v((ITERS, k, 2 * k), F32), v((ITERS, 3, k, 2 * k), F32),
        v((2 * chunks, k, step), F32), v((na, k), F32), v((na, k), F32), v((na, k), F32),
        v((n_pix, na, k), F32), v((192, k), F32),
        sem(), sem(), sem(n_pix), sem(3), sem(3), sem(ITERS + 1, chunks), sem(ITERS),
        sem(ITERS, GROUP), sem(ITERS, n_hi), sem(ITERS, GROUP), sem(ITERS), sem(ITERS, 3),
        sem(chunks), sem(), sem(n_pix),
    ]
    return pl.pallas_call(
        functools.partial(kernel, n_pix),
        out_shape=(
            jax.ShapeDtypeStruct((k, pixels), F32),
            jax.ShapeDtypeStruct((na, pixels), F32),
        ),
        in_specs=[vmem] * 3,
        out_specs=(vmem, vmem),
        scratch_shapes=scratch,
        compiler_params=pltpu.CompilerParams(
            collective_id=0, has_side_effects=True, vmem_limit_bytes=48 * 1024 * 1024
        ),
    )(spectra, start, spread)


def solution(mesh):
    placed = (P("pix", "chan"), P(None, "chan"), P())
    return jax.shard_map(
        functools.partial(local, mesh.shape["pix"]),
        mesh=mesh,
        in_specs=placed,
        out_specs=(P(None, "pix"), P(None, "pix")),
        check_vma=False,
    )
```

```python
import functools

import jax
import jax.numpy as jnp
from jax import lax
from jax.experimental import pallas as pl
from jax.experimental.pallas import tpu as pltpu
from jax.sharding import PartitionSpec as P

ITERS = 5
GROUP = 8
MESH = pl.DeviceIdType.MESH
HIGH = lax.Precision.HIGHEST
F32 = jnp.float32
BF16 = jnp.bfloat16
NT = (((1,), (1,)), ((), ()))


def dot(a, b, dims=(((1,), (0,)), ((), ())), precision=None):
    return lax.dot_general(a, b, dims, precision=precision, preferred_element_type=F32)


def inverse_factor(gram):
    n = gram.shape[0]
    rows = lax.broadcasted_iota(jnp.int32, (n, 128), 0)
    lanes = lax.broadcasted_iota(jnp.int32, (n, 128), 1)
    full = jnp.where(lanes < 64, jnp.where(lanes == rows, 1.0, 0.0), gram)
    sub = lax.broadcasted_iota(jnp.int32, (8, 128), 0)
    count = n // 8
    blocks = [full[8 * i : 8 * i + 8, :] for i in range(count)]
    done = []
    for home in range(count):
        spread = [
            [jnp.broadcast_to(block[:, at : at + 1], (8, 128))
             for at in range(64 + 8 * home, 72 + 8 * home)]
            for block in blocks
        ]
        pivots = jnp.ones((8, 128), F32)
        for r in range(8):
            inverse = 1.0 / spread[0][r][r : r + 1, :]
            pivots = jnp.where(sub == r, spread[0][r], pivots)
            line = blocks[0][r : r + 1, :] * inverse
            later = {c: spread[0][c][r : r + 1, :] * inverse for c in range(r + 1, 8)}
            for i in range(len(blocks)):
                ratio = spread[i][r]
                if i == 0:
                    ratio = jnp.where(sub > r, ratio, 0.0)
                for c, value in later.items():
                    spread[i][c] = spread[i][c] - ratio * value
                blocks[i] = blocks[i] - ratio * line
        done.append(blocks[0] * lax.rsqrt(pivots))
        blocks = blocks[1:]
    return jnp.where(lanes < 64, jnp.concatenate(done, axis=0), 0.0)


def kernel(
    n_pix, s_ref, start_ref, anchors_ref, scores_ref, abund_ref,
    other_s, start_in, col_out, col_in, col_mine, col_chan, row_out, row_in, row_sum,
    w, wt, load, x_out, x_in, acc, half_in, keep, rs_in, hi_in, ag, back_in, padded,
    gram_out, gram_in, score, rows_half, rows_half_in, rows_out, rows_in, rows_pad,
    s_sem, st_sem, col_sem, cc_sem, row_sem, x_sem, half_sem, rs_sem, hi_sem, ag_sem,
    bk_sem, gram_sem, sc_sem, rh_sem, rows_sem,
):
    pix = lax.axis_index("pix")
    chan = lax.axis_index("chan")
    lo, hi = lax.rem(chan, 2), lax.div(chan, 2)
    mates = [hi * 2 + 1 - lo, (1 - hi) * 2 + lo, (1 - hi) * 2 + 1 - lo]
    low = lax.rem(pix, GROUP)
    base = pix - low
    n_hi = n_pix // GROUP
    k_rows, ch = start_ref.shape
    pixels = s_ref.shape[0]
    half = pixels // 2
    step_pix = x_out.shape[-1]
    chunks = half // step_pix

    def send(src, dst, sems, device):
        return pltpu.make_async_remote_copy(
            src_ref=src, dst_ref=dst, send_sem=sems.at[0], recv_sem=sems.at[1],
            device_id=device, device_id_type=MESH,
        )

    def all_pix(f):
        def body(d, carry):
            f(d, lax.rem(pix + d, n_pix))
            return carry
        lax.fori_loop(1, n_pix, body, 0)

    barrier = pltpu.get_barrier_semaphore()
    for mate in mates:
        pl.semaphore_signal(barrier, inc=1, device_id=(pix, mate), device_id_type=MESH)
    all_pix(lambda d, to: pl.semaphore_signal(
        barrier, inc=1, device_id=(to, chan), device_id_type=MESH))
    pl.semaphore_wait(barrier, 3 + n_pix - 1)

    away = pl.multiple_of((1 - lo) * half, half)
    swap = send(s_ref.at[pl.ds(away, half)], other_s, s_sem, (pix, mates[0]))
    swap.start()
    swap_start = send(start_ref, start_in, st_sem, (pix, mates[0]))
    swap_start.start()

    ones = jnp.ones((8, step_pix), BF16)
    total_col = jnp.zeros((8, ch), F32)
    for j in range(2 * chunks):
        total_col += dot(ones, s_ref[j * step_pix : (j + 1) * step_pix, :])
    col_out[...] = total_col

    def col_copy(d, to):
        return send(col_out, col_in.at[d], col_sem.at[d], (to, chan))
    all_pix(lambda d, to: col_copy(d, to).start())

    ones_ch = jnp.ones((8, ch), BF16)
    for j in range(2 * chunks):
        sums = dot(ones_ch, s_ref[j * step_pix : (j + 1) * step_pix, :], NT)
        row_out[j : j + 1, :] = sums[0:1, :]
    row_copies = [
        send(row_out, row_in.at[m], row_sem.at[m], (pix, mates[m])) for m in range(3)
    ]
    for copy in row_copies:
        copy.start()

    col_in[0] = col_out[...]
    all_pix(lambda d, to: col_copy(d, to).wait())
    col_mine[...] = jnp.sum(col_in[...], axis=0)
    col_copies = [
        send(col_mine, col_chan.at[m], cc_sem.at[m], (pix, mates[m])) for m in range(3)
    ]
    for copy in col_copies:
        copy.start()
    for copy in row_copies:
        copy.wait()
    sums = (row_out[...] + row_in[0]) + (row_in[1] + row_in[2])
    for j in range(2 * chunks):
        row_sum[j] = jnp.broadcast_to(sums[j : j + 1, :], (8, step_pix))
    for copy in col_copies:
        copy.wait()
    cols = (col_mine[0:1, :] + col_chan[0, 0:1, :]) + (
        col_chan[1, 0:1, :] + col_chan[2, 0:1, :])
    inv_total = 1.0 / jnp.sum(cols, axis=1, keepdims=True)
    shares = [col_mine[0:1, :] * inv_total, col_chan[0, 0:1, :] * inv_total]
    swap.wait()

    tiles = step_pix // 128

    def weigh(i, carry):
        j, q = lax.div(i, tiles), lax.rem(i, tiles)
        first = pl.multiple_of(q * 128, 128)
        line = row_sum[lo * chunks + j, 0:1, pl.ds(first, 128)]
        wide = jnp.transpose(jnp.broadcast_to(line, (128, 128)))
        mine = s_ref[pl.ds(pl.multiple_of(lo * half + i * 128, 128), 128), :]
        theirs = other_s[pl.ds(pl.multiple_of(i * 128, 128), 128), :]
        for side, counts in enumerate((mine, theirs)):
            for g in range(ch // 128):
                expect = wide * shares[side][:, g * 128 : (g + 1) * 128]
                value = counts[:, g * 128 : (g + 1) * 128].astype(F32)
                weighted = (value - expect) * lax.rsqrt(expect)
                at = side * ch + g * 128
                w[j, pl.ds(first, 128), at : at + 128] = weighted.astype(BF16)
                wt[j, at : at + 128, pl.ds(first, 128)] = jnp.transpose(weighted).astype(BF16)
        return carry
    lax.fori_loop(0, chunks * tiles, weigh, 0)

    swap_start.wait()
    load[:, :ch] = start_ref[...]
    load[:, ch:] = start_in[...]
    padded[...] = jnp.zeros_like(padded)
    rows_pad[...] = jnp.zeros_like(rows_pad)

    def x_copy(t, j):
        return send(x_out.at[t, j], x_in.at[t, j], x_sem.at[t, j], (pix, mates[1]))

    def project(t):
        def body(j, carry):
            x_out[t, j] = dot(load[...], wt[j]).astype(BF16)
            x_copy(t, j).start()
            return carry
        lax.fori_loop(0, chunks, body, 0)

    def gather(t, j):
        x_copy(t, j).wait()
        return x_out[t, j].astype(F32) + x_in[t, j].astype(F32)

    per = k_rows // GROUP

    def iteration(t, carry):
        project(t)
        acc[...] = jnp.zeros_like(acc)

        def body(j, carry):
            acc[...] += dot(gather(t, j).astype(BF16), w[j])
            return carry
        lax.fori_loop(0, chunks, body, 0)

        keep[t, 0] = acc[:, ch:]
        copy = send(keep.at[t, 0], half_in.at[t], half_sem.at[t], (pix, mates[0]))
        copy.start()
        copy.wait()
        keep[t, 1] = acc[:, :ch] + half_in[t]

        def partner(d):
            return lax.rem(low + d, GROUP)
        spread = [
            send(
                keep.at[t, 1, pl.ds(pl.multiple_of(partner(d) * per, per), per)],
                rs_in.at[t, d], rs_sem.at[t, d], (base + partner(d), chan))
            for d in range(1, GROUP)
        ]
        for copy in spread:
            copy.start()
        slab = keep[t, 1, pl.ds(pl.multiple_of(low * per, per), per), :]
        for d, copy in enumerate(spread, 1):
            copy.wait()
            slab = slab + rs_in[t, d]
        if n_hi > 1:
            hi_in[t, 0] = slab
            across = [
                send(hi_in.at[t, 0], hi_in.at[t, e], hi_sem.at[t, e],
                     (lax.rem(pix + e * GROUP, n_pix), chan))
                for e in range(1, n_hi)
            ]
            for copy in across:
                copy.start()
            for copy in across:
                copy.wait()
            slab = hi_in[t, lax.rem(n_hi + lax.div(pix, GROUP), n_hi)]
            for e in range(1, n_hi):
                slab = slab + hi_in[t, lax.rem(n_hi + lax.div(pix, GROUP) - e, n_hi)]
        mine = pl.ds(pl.multiple_of(low * per, per), per)
        ag[t, mine] = slab
        collect = [
            send(ag.at[t, mine], ag.at[t, mine], ag_sem.at[t, d], (base + partner(d), chan))
            for d in range(1, GROUP)
        ]
        for copy in collect:
            copy.start()
        for copy in collect:
            copy.wait()
        twin = send(ag.at[t], back_in.at[t], bk_sem.at[t], (pix, mates[0]))
        twin.start()
        back = ag[t]
        padded[k_rows : 2 * k_rows, :ch] = back
        gram_out[t] = dot(back[: k_rows // 2], padded[k_rows:, :ch], NT, HIGH) + dot(
            back[k_rows // 2 :], padded[: 2 * k_rows, :ch], NT, HIGH)
        grams = [
            send(gram_out.at[t], gram_in.at[t, m], gram_sem.at[t, m], (pix, mates[m]))
            for m in range(3)
        ]
        for copy in grams:
            copy.start()
        for copy in grams:
            copy.wait()
        gram = (gram_out[t] + gram_in[t, 0]) + (gram_in[t, 1] + gram_in[t, 2])
        factor = inverse_factor(jnp.concatenate([pltpu.roll(gram, 64, 1), gram], axis=0))
        twin.wait()
        padded[k_rows : 2 * k_rows, ch:] = back_in[t]
        load[...] = dot(factor, padded[k_rows:, :], precision=HIGH).astype(BF16)
        return carry
    lax.fori_loop(0, ITERS, iteration, 0)

    project(ITERS)
    n_anchor = anchors_ref.shape[0]
    wanted = anchors_ref[...][:, :1] - pix * pixels - lo * half
    rows_half[...] = jnp.zeros_like(rows_half)

    def finish(j, carry):
        value = gather(ITERS, j)
        slot = lo * chunks + j
        score[slot] = value
        send(score.at[slot], score.at[slot], sc_sem.at[j], (pix, mates[0])).start()
        positions = lax.broadcasted_iota(jnp.int32, (n_anchor, step_pix), 1)
        picks = jnp.where(positions == wanted - j * step_pix, 1.0, 0.0)
        rows_half[...] += dot(picks, value, NT, HIGH)
        return carry
    lax.fori_loop(0, chunks, finish, 0)
    pair_rows = send(rows_half, rows_half_in, rh_sem, (pix, mates[0]))
    pair_rows.start()
    pair_rows.wait()
    rows_out[...] = rows_half[...] + rows_half_in[...]

    def rows_copy(d, to):
        return send(rows_out, rows_in.at[d], rows_sem.at[d], (to, chan))
    all_pix(lambda d, to: rows_copy(d, to).start())
    rows_in[0] = rows_out[...]
    for j in range(chunks):
        slot = lo * chunks + j
        send(score.at[slot], score.at[slot], sc_sem.at[j], (pix, mates[0])).wait()
    for j in range(2 * chunks):
        scores_ref[:, j * step_pix : (j + 1) * step_pix] = score[j]
    all_pix(lambda d, to: rows_copy(d, to).wait())
    rows = jnp.sum(rows_in[...], axis=0)
    rows_pad[64 : 64 + n_anchor, :] = rows
    small = dot(rows, rows_pad[0:128, :], NT, HIGH)
    factor = inverse_factor(small)
    solved = dot(factor, rows_pad[64:192, :], precision=HIGH)
    both = dot(jnp.transpose(factor)[:n_anchor, :], solved, precision=HIGH)
    for j in range(2 * chunks):
        abund_ref[:, j * step_pix : (j + 1) * step_pix] = dot(both, score[j], precision=HIGH)


def local(n_pix, spectra, start, anchors):
    pixels, ch = spectra.shape
    k = start.shape[0]
    na = anchors.shape[0]
    half = pixels // 2
    step = min(512, half)
    chunks = half // step
    n_hi = n_pix // GROUP
    spread = jnp.broadcast_to(anchors[:, None], (na, 128))
    vmem = pl.BlockSpec(memory_space=pltpu.VMEM)
    v = pltpu.VMEM
    sem = lambda *shape: pltpu.SemaphoreType.DMA(tuple(shape) + (2,))
    scratch = [
        v((half, ch), BF16), v((k, ch), BF16), v((8, ch), F32), v((n_pix, 8, ch), F32),
        v((8, ch), F32), v((3, 8, ch), F32), v((2 * chunks, step), F32),
        v((3, 2 * chunks, step), F32), v((2 * chunks, 8, step), F32),
        v((chunks, step, 2 * ch), BF16), v((chunks, 2 * ch, step), BF16), v((k, 2 * ch), BF16),
        v((ITERS + 1, chunks, k, step), BF16), v((ITERS + 1, chunks, k, step), BF16),
        v((k, 2 * ch), F32), v((ITERS, k, ch), F32), v((ITERS, 2, k, ch), F32),
        v((ITERS, GROUP, k // GROUP, ch), F32), v((ITERS, n_hi, k // GROUP, ch), F32),
        v((ITERS, k, ch), F32), v((ITERS, k, ch), F32), v((3 * k, 2 * ch), F32),
        v((ITERS, k // 2, 2 * k), F32), v((ITERS, 3, k // 2, 2 * k), F32),
        v((2 * chunks, k, step), F32), v((na, k), F32), v((na, k), F32), v((na, k), F32),
        v((n_pix, na, k), F32), v((192, k), F32),
        sem(), sem(), sem(n_pix), sem(3), sem(3), sem(ITERS + 1, chunks), sem(ITERS),
        sem(ITERS, GROUP), sem(ITERS, n_hi), sem(ITERS, GROUP), sem(ITERS), sem(ITERS, 3),
        sem(chunks), sem(), sem(n_pix),
    ]
    return pl.pallas_call(
        functools.partial(kernel, n_pix),
        out_shape=(
            jax.ShapeDtypeStruct((k, pixels), F32),
            jax.ShapeDtypeStruct((na, pixels), F32),
        ),
        in_specs=[vmem] * 3,
        out_specs=(vmem, vmem),
        scratch_shapes=scratch,
        compiler_params=pltpu.CompilerParams(
            collective_id=0, has_side_effects=True, vmem_limit_bytes=48 * 1024 * 1024
        ),
    )(spectra, start, spread)


def solution(mesh):
    placed = (P("pix", "chan"), P(None, "chan"), P())
    return jax.shard_map(
        functools.partial(local, mesh.shape["pix"]),
        mesh=mesh,
        in_specs=placed,
        out_specs=(P(None, "pix"), P(None, "pix")),
        check_vma=False,
    )
```

```python
import functools

import jax
import jax.numpy as jnp
from jax import lax
from jax.experimental import pallas as pl
from jax.experimental.pallas import tpu as pltpu
from jax.sharding import PartitionSpec as P

ITERS = 5
GROUP = 8
MESH = pl.DeviceIdType.MESH
HIGH = lax.Precision.HIGHEST
F32 = jnp.float32
BF16 = jnp.bfloat16
NT = (((1,), (1,)), ((), ()))


def dot(a, b, dims=(((1,), (0,)), ((), ())), precision=None):
    return lax.dot_general(a, b, dims, precision=precision, preferred_element_type=F32)


def inverse_factor(gram):
    n = gram.shape[0]
    rows = lax.broadcasted_iota(jnp.int32, (n, 128), 0)
    lanes = lax.broadcasted_iota(jnp.int32, (n, 128), 1)
    full = jnp.where(lanes < 64, jnp.where(lanes == rows, 1.0, 0.0), gram)
    sub = lax.broadcasted_iota(jnp.int32, (8, 128), 0)
    count = n // 8
    blocks = [full[8 * i : 8 * i + 8, :] for i in range(count)]
    done = []
    for home in range(count):
        spread = [
            [jnp.broadcast_to(block[:, at : at + 1], (8, 128))
             for at in range(64 + 8 * home, 72 + 8 * home)]
            for block in blocks
        ]
        pivots = jnp.ones((8, 128), F32)
        for r in range(8):
            inverse = 1.0 / spread[0][r][r : r + 1, :]
            pivots = jnp.where(sub == r, spread[0][r], pivots)
            line = blocks[0][r : r + 1, :] * inverse
            later = {c: spread[0][c][r : r + 1, :] * inverse for c in range(r + 1, 8)}
            for i in range(len(blocks)):
                ratio = spread[i][r]
                if i == 0:
                    ratio = jnp.where(sub > r, ratio, 0.0)
                for c, value in later.items():
                    spread[i][c] = spread[i][c] - ratio * value
                blocks[i] = blocks[i] - ratio * line
        done.append(blocks[0] * lax.rsqrt(pivots))
        blocks = blocks[1:]
    return jnp.where(lanes < 64, jnp.concatenate(done, axis=0), 0.0)


def split_rows(ref, value, lanes):
    top = value.astype(BF16)
    n = value.shape[0]
    ref[:n, lanes] = top
    ref[n:, lanes] = (value - top.astype(F32)).astype(BF16)


def split_dot(left, pair):
    top = left.astype(BF16)
    low = (left - top.astype(F32)).astype(BF16)
    twice = (top.astype(F32) + pltpu.roll(top.astype(F32), 64, 1)).astype(BF16)
    n = left.shape[0]
    out = dot(jnp.concatenate([twice, low], axis=0), pair)
    return out[:n] + out[n:]


def kernel(
    n_pix, s_hbm, start_ref, anchors_ref, scores_ref, abund_ref,
    s_ref, other_s, start_in, col_out, col_in, col_mine, col_chan, row_out, row_in, row_sum,
    w, wt, load, x_out, x_in, acc, half_in, keep, rs_in, hi_in, ag, back_in, padded,
    gram_out, gram_in, score, rows_half, rows_half_in, rows_out, rows_in, rows_pad,
    halves, pieces, in_sem, s_sem, st_sem, col_sem, cc_sem, row_sem, x_sem, half_sem, rs_sem, hi_sem, ag_sem,
    bk_sem, gram_sem, sc_sem, rh_sem, rows_sem,
):
    pix = lax.axis_index("pix")
    chan = lax.axis_index("chan")
    lo, hi = lax.rem(chan, 2), lax.div(chan, 2)
    mates = [hi * 2 + 1 - lo, (1 - hi) * 2 + lo, (1 - hi) * 2 + 1 - lo]
    low = lax.rem(pix, GROUP)
    base = pix - low
    n_hi = n_pix // GROUP
    k_rows, ch = start_ref.shape
    pixels = s_ref.shape[0]
    half = pixels // 2
    step_pix = x_out.shape[-1]
    chunks = half // step_pix

    def send(src, dst, sems, device):
        return pltpu.make_async_remote_copy(
            src_ref=src, dst_ref=dst, send_sem=sems.at[0], recv_sem=sems.at[1],
            device_id=device, device_id_type=MESH,
        )

    def all_pix(f):
        def body(d, carry):
            f(d, lax.rem(pix + d, n_pix))
            return carry
        lax.fori_loop(1, n_pix, body, 0)

    loads = []
    for j in range(2 * chunks):
        part = pl.ds(j * step_pix, step_pix)
        loads.append(pltpu.make_async_copy(s_hbm.at[part], s_ref.at[part], in_sem.at[j]))
        loads[-1].start()

    barrier = pltpu.get_barrier_semaphore()
    for mate in mates:
        pl.semaphore_signal(barrier, inc=1, device_id=(pix, mate), device_id_type=MESH)
    all_pix(lambda d, to: pl.semaphore_signal(
        barrier, inc=1, device_id=(to, chan), device_id_type=MESH))
    pl.semaphore_wait(barrier, 3 + n_pix - 1)

    away = pl.multiple_of((1 - lo) * half, half)
    swap = send(s_hbm.at[pl.ds(away, half)], other_s, s_sem, (pix, mates[0]))
    swap.start()
    swap_start = send(start_ref, start_in, st_sem, (pix, mates[0]))
    swap_start.start()

    total_col = jnp.zeros((8, ch), F32)
    for j in range(2 * chunks):
        loads[j].wait()
        block = s_ref[j * step_pix : (j + 1) * step_pix, :].astype(F32)
        total_col += jnp.sum(block.reshape(step_pix // 8, 8, ch), axis=0)
    col_out[...] = jnp.sum(total_col, axis=0, keepdims=True)

    def col_copy(d, to):
        return send(col_out, col_in.at[d], col_sem.at[d], (to, chan))
    all_pix(lambda d, to: col_copy(d, to).start())

    ones = jnp.ones((ch, 128), BF16)
    diagonal = lax.broadcasted_iota(jnp.int32, (128, 128), 0) == (
        lax.broadcasted_iota(jnp.int32, (128, 128), 1))
    for j in range(2 * chunks):
        sums = dot(s_ref[j * step_pix : (j + 1) * step_pix, :], ones)
        for b in range(step_pix // 128):
            square = jnp.where(diagonal, sums[b * 128 : (b + 1) * 128, :], 0.0)
            row_out[j : j + 1, b * 128 : (b + 1) * 128] = jnp.sum(
                square, axis=0, keepdims=True)
    row_copies = [
        send(row_out, row_in.at[m], row_sem.at[m], (pix, mates[m])) for m in range(3)
    ]
    for copy in row_copies:
        copy.start()

    col_in[0] = col_out[...]
    all_pix(lambda d, to: col_copy(d, to).wait())
    col_mine[...] = jnp.sum(col_in[...], axis=0)
    col_copies = [
        send(col_mine, col_chan.at[m], cc_sem.at[m], (pix, mates[m])) for m in range(3)
    ]
    for copy in col_copies:
        copy.start()
    for copy in row_copies:
        copy.wait()
    sums = (row_out[...] + row_in[0]) + (row_in[1] + row_in[2])
    for j in range(2 * chunks):
        row_sum[j] = jnp.broadcast_to(sums[j : j + 1, :], (8, step_pix))
    for copy in col_copies:
        copy.wait()
    cols = (col_mine[...] + col_chan[0]) + (col_chan[1] + col_chan[2])
    inv_total = 1.0 / jnp.sum(cols, axis=1, keepdims=True)
    shares = [col_mine[...] * inv_total, col_chan[0] * inv_total]
    share_roots = [lax.rsqrt(share) for share in shares]
    swap.wait()

    tiles = step_pix // 128

    def weigh(i, carry):
        j, q = lax.div(i, tiles), lax.rem(i, tiles)
        first = pl.multiple_of(q * 128, 128)
        line = row_sum[lo * chunks + j, 0:1, pl.ds(first, 128)]
        wide = jnp.transpose(jnp.broadcast_to(line, (128, 128)))
        wide_root = lax.rsqrt(wide)
        mine = s_ref[pl.ds(pl.multiple_of(lo * half + i * 128, 128), 128), :]
        theirs = other_s[pl.ds(pl.multiple_of(i * 128, 128), 128), :]
        for side, counts in enumerate((mine, theirs)):
            for g in range(ch // 128):
                lanes = slice(g * 128, (g + 1) * 128)
                expect = wide * shares[side][:, lanes]
                root = wide_root * share_roots[side][:, lanes]
                value = counts[:, lanes].astype(F32)
                weighted = ((value - expect) * root).astype(BF16)
                at = side * ch + g * 128
                w[j, pl.ds(first, 128), at : at + 128] = weighted
                wt[j, at : at + 128, pl.ds(first, 128)] = jnp.transpose(weighted)
        return carry
    lax.fori_loop(0, chunks * tiles, weigh, 0)

    swap_start.wait()
    load[:, :ch] = start_ref[...]
    load[:, ch:] = start_in[...]
    padded[...] = jnp.zeros_like(padded)
    rows_pad[...] = jnp.zeros_like(rows_pad)

    def x_copy(t, j):
        return send(x_out.at[t, j], x_in.at[t, j], x_sem.at[t, j], (pix, mates[1]))

    def project(t):
        def body(j, carry):
            x_out[t, j] = dot(load[...], wt[j]).astype(BF16)
            x_copy(t, j).start()
            return carry
        lax.fori_loop(0, chunks, body, 0)

    def gather(t, j):
        x_copy(t, j).wait()
        return x_out[t, j].astype(F32) + x_in[t, j].astype(F32)

    per = k_rows // GROUP

    def iteration(t, carry):
        project(t)
        acc[...] = jnp.zeros_like(acc)

        def body(j, carry):
            acc[...] += dot(gather(t, j).astype(BF16), w[j])
            return carry
        lax.fori_loop(0, chunks, body, 0)

        keep[t, 0] = acc[:, ch:]
        copy = send(keep.at[t, 0], half_in.at[t], half_sem.at[t], (pix, mates[0]))
        copy.start()
        copy.wait()
        keep[t, 1] = acc[:, :ch] + half_in[t]

        def partner(d):
            return lax.rem(low + d, GROUP)
        spread = [
            send(
                keep.at[t, 1, pl.ds(pl.multiple_of(partner(d) * per, per), per)],
                rs_in.at[t, d], rs_sem.at[t, d], (base + partner(d), chan))
            for d in range(1, GROUP)
        ]
        for copy in spread:
            copy.start()
        slab = keep[t, 1, pl.ds(pl.multiple_of(low * per, per), per), :]
        for d, copy in enumerate(spread, 1):
            copy.wait()
            slab = slab + rs_in[t, d]
        if n_hi > 1:
            hi_in[t, 0] = slab
            across = [
                send(hi_in.at[t, 0], hi_in.at[t, e], hi_sem.at[t, e],
                     (lax.rem(pix + e * GROUP, n_pix), chan))
                for e in range(1, n_hi)
            ]
            for copy in across:
                copy.start()
            for copy in across:
                copy.wait()
            slab = hi_in[t, lax.rem(n_hi + lax.div(pix, GROUP), n_hi)]
            for e in range(1, n_hi):
                slab = slab + hi_in[t, lax.rem(n_hi + lax.div(pix, GROUP) - e, n_hi)]
        mine = pl.ds(pl.multiple_of(low * per, per), per)
        ag[t, mine] = slab
        collect = [
            send(ag.at[t, mine], ag.at[t, mine], ag_sem.at[t, d], (base + partner(d), chan))
            for d in range(1, GROUP)
        ]
        for copy in collect:
            copy.start()
        for copy in collect:
            copy.wait()
        twin = send(ag.at[t], back_in.at[t], bk_sem.at[t], (pix, mates[0]))
        twin.start()
        back = ag[t]
        padded[k_rows : 2 * k_rows, :] = back
        split_rows(halves, back, slice(0, ch))
        gram_out[t] = dot(back[: k_rows // 2], padded[k_rows:, :], NT, HIGH) + dot(
            back[k_rows // 2 :], padded[: 2 * k_rows, :], NT, HIGH)
        grams = [
            send(gram_out.at[t], gram_in.at[t, m], gram_sem.at[t, m], (pix, mates[m]))
            for m in range(3)
        ]
        for copy in grams:
            copy.start()
        for copy in grams:
            copy.wait()
        gram = (gram_out[t] + gram_in[t, 0]) + (gram_in[t, 1] + gram_in[t, 2])
        factor = inverse_factor(jnp.concatenate([pltpu.roll(gram, 64, 1), gram], axis=0))
        twin.wait()
        split_rows(halves, back_in[t], slice(ch, 2 * ch))
        load[...] = split_dot(factor, halves[...]).astype(BF16)
        return carry
    lax.fori_loop(0, ITERS, iteration, 0)

    project(ITERS)
    n_anchor = anchors_ref.shape[0]
    order = lax.broadcasted_iota(jnp.int32, (n_anchor, step_pix), 0)
    wanted = jnp.zeros((n_anchor, step_pix), jnp.int32)
    for a in range(n_anchor):
        wanted = jnp.where(order == a, anchors_ref[a], wanted)
    wanted = wanted - pix * pixels - lo * half
    rows_half[...] = jnp.zeros_like(rows_half)

    def finish(j, carry):
        value = gather(ITERS, j)
        slot = lo * chunks + j
        score[slot] = value
        send(score.at[slot], score.at[slot], sc_sem.at[j], (pix, mates[0])).start()
        positions = lax.broadcasted_iota(jnp.int32, (n_anchor, step_pix), 1)
        picks = jnp.where(positions == wanted - j * step_pix, 1.0, 0.0)
        rows_half[...] += dot(picks, value, NT, HIGH)
        return carry
    lax.fori_loop(0, chunks, finish, 0)
    pair_rows = send(rows_half, rows_half_in, rh_sem, (pix, mates[0]))
    pair_rows.start()
    pair_rows.wait()
    rows_out[...] = rows_half[...] + rows_half_in[...]

    def rows_copy(d, to):
        return send(rows_out, rows_in.at[d], rows_sem.at[d], (to, chan))
    all_pix(lambda d, to: rows_copy(d, to).start())
    rows_in[0] = rows_out[...]
    for j in range(chunks):
        slot = lo * chunks + j
        send(score.at[slot], score.at[slot], sc_sem.at[j], (pix, mates[0])).wait()
    for j in range(2 * chunks):
        part = slice(j * step_pix, (j + 1) * step_pix)
        scores_ref[:, part] = score[j]
        split_rows(pieces, score[j], part)
    all_pix(lambda d, to: rows_copy(d, to).wait())
    rows = jnp.sum(rows_in[...], axis=0)
    rows_pad[64 : 64 + n_anchor, :k_rows] = rows
    small = dot(rows_pad[64 : 64 + n_anchor, :], rows_pad[0:128, :], NT, HIGH)
    factor = inverse_factor(small)
    solved = dot(factor, rows_pad[64:192, :], precision=HIGH)
    both = dot(jnp.transpose(factor)[:n_anchor, :], solved, precision=HIGH)
    abund_ref[...] = split_dot(both, pieces[...])


def local(n_pix, spectra, start, anchors):
    pixels, ch = spectra.shape
    k = start.shape[0]
    na = anchors.shape[0]
    half = pixels // 2
    step = min(512, half)
    chunks = half // step
    n_hi = n_pix // GROUP
    vmem = pl.BlockSpec(memory_space=pltpu.VMEM)
    smem = pl.BlockSpec(memory_space=pltpu.SMEM)
    hbm = pl.BlockSpec(memory_space=pl.ANY)
    v = pltpu.VMEM
    sem = lambda *shape: pltpu.SemaphoreType.DMA(tuple(shape) + (2,))
    scratch = [
        v((pixels, ch), BF16), v((half, ch), BF16), v((k, ch), BF16), v((1, ch), F32),
        v((n_pix, 1, ch), F32), v((1, ch), F32), v((3, 1, ch), F32), v((2 * chunks, step), F32),
        v((3, 2 * chunks, step), F32), v((2 * chunks, 8, step), F32),
        v((chunks, step, 2 * ch), BF16), v((chunks, 2 * ch, step), BF16), v((k, 2 * ch), BF16),
        v((ITERS + 1, chunks, k, step), BF16), v((ITERS + 1, chunks, k, step), BF16),
        v((k, 2 * ch), F32), v((ITERS, k, ch), F32), v((ITERS, 2, k, ch), F32),
        v((ITERS, GROUP, k // GROUP, ch), F32), v((ITERS, n_hi, k // GROUP, ch), F32),
        v((ITERS, k, ch), F32), v((ITERS, k, ch), F32), v((3 * k, ch), F32),
        v((ITERS, k // 2, 2 * k), F32), v((ITERS, 3, k // 2, 2 * k), F32),
        v((2 * chunks, k, step), F32), v((na, k), F32), v((na, k), F32), v((na, k), F32),
        v((n_pix, na, k), F32), v((192, 128), F32),
        v((2 * k, 2 * ch), BF16), v((2 * k, pixels), BF16),
        pltpu.SemaphoreType.DMA((2 * chunks,)), sem(), sem(), sem(n_pix), sem(3), sem(3), sem(ITERS + 1, chunks), sem(ITERS),
        sem(ITERS, GROUP), sem(ITERS, n_hi), sem(ITERS, GROUP), sem(ITERS), sem(ITERS, 3),
        sem(chunks), sem(), sem(n_pix),
    ]
    return pl.pallas_call(
        functools.partial(kernel, n_pix),
        out_shape=(
            jax.ShapeDtypeStruct((k, pixels), F32),
            jax.ShapeDtypeStruct((na, pixels), F32),
        ),
        in_specs=[hbm, vmem, smem],
        out_specs=(vmem, vmem),
        scratch_shapes=scratch,
        compiler_params=pltpu.CompilerParams(
            collective_id=0, has_side_effects=True, vmem_limit_bytes=60 * 1024 * 1024
        ),
    )(spectra, start, anchors)


def solution(mesh):
    placed = (P("pix", "chan"), P(None, "chan"), P())
    return jax.shard_map(
        functools.partial(local, mesh.shape["pix"]),
        mesh=mesh,
        in_specs=placed,
        out_specs=(P(None, "pix"), P(None, "pix")),
        check_vma=False,
    )
```

```python
import functools

import jax
import jax.numpy as jnp
from jax import lax
from jax.experimental import pallas as pl
from jax.experimental.pallas import tpu as pltpu
from jax.sharding import PartitionSpec as P

ITERS = 5
GROUP = 8
MESH = pl.DeviceIdType.MESH
HIGH = lax.Precision.HIGHEST
F32 = jnp.float32
BF16 = jnp.bfloat16
NT = (((1,), (1,)), ((), ()))


def dot(a, b, dims=(((1,), (0,)), ((), ())), precision=None):
    return lax.dot_general(a, b, dims, precision=precision, preferred_element_type=F32)


def inverse_factor(gram):
    n = gram.shape[0]
    rows = lax.broadcasted_iota(jnp.int32, (n, 128), 0)
    lanes = lax.broadcasted_iota(jnp.int32, (n, 128), 1)
    full = jnp.where(lanes < 64, jnp.where(lanes == rows, 1.0, 0.0), gram)
    sub = lax.broadcasted_iota(jnp.int32, (8, 128), 0)
    count = n // 8
    blocks = [full[8 * i : 8 * i + 8, :] for i in range(count)]
    done = []
    for home in range(count):
        spread = [
            [jnp.broadcast_to(block[:, at : at + 1], (8, 128))
             for at in range(64 + 8 * home, 72 + 8 * home)]
            for block in blocks
        ]
        pivots = jnp.ones((8, 128), F32)
        for r in range(8):
            inverse = 1.0 / spread[0][r][r : r + 1, :]
            pivots = jnp.where(sub == r, spread[0][r], pivots)
            line = blocks[0][r : r + 1, :] * inverse
            later = {c: spread[0][c][r : r + 1, :] * inverse for c in range(r + 1, 8)}
            for i in range(len(blocks)):
                ratio = spread[i][r]
                if i == 0:
                    ratio = jnp.where(sub > r, ratio, 0.0)
                for c, value in later.items():
                    spread[i][c] = spread[i][c] - ratio * value
                blocks[i] = blocks[i] - ratio * line
        done.append(blocks[0] * lax.rsqrt(pivots))
        blocks = blocks[1:]
    return jnp.where(lanes < 64, jnp.concatenate(done, axis=0), 0.0)


def split_rows(ref, value, lanes):
    top = value.astype(BF16)
    n = value.shape[0]
    ref[:n, lanes] = top
    ref[n:, lanes] = (value - top.astype(F32)).astype(BF16)


def split_dot(left, pair):
    top = left.astype(BF16)
    low = (left - top.astype(F32)).astype(BF16)
    twice = (top.astype(F32) + pltpu.roll(top.astype(F32), 64, 1)).astype(BF16)
    n = left.shape[0]
    out = dot(jnp.concatenate([twice, low], axis=0), pair)
    return out[:n] + out[n:]


def kernel(
    n_pix, s_hbm, start_ref, anchors_ref, scores_ref, abund_ref,
    s_ref, other_s, start_in, col_out, col_in, col_mine, col_chan, row_out, row_in, row_sum,
    w, wt, load, x_out, x_in, acc, mate_out, half_in, keep, rs_in, hi_in, ag, back_in, padded,
    gram_out, gram_in, score, rows_half, rows_half_in, rows_out, rows_in, rows_pad,
    halves, theirs, pieces, in_sem, s_sem, st_sem, col_sem, cc_sem, row_sem, x_sem, half_sem, rs_sem, hi_sem, ag_sem,
    bk_sem, gram_sem, sc_sem, rh_sem, rows_sem,
):
    pix = lax.axis_index("pix")
    chan = lax.axis_index("chan")
    lo, hi = lax.rem(chan, 2), lax.div(chan, 2)
    mates = [hi * 2 + 1 - lo, (1 - hi) * 2 + lo, (1 - hi) * 2 + 1 - lo]
    low = lax.rem(pix, GROUP)
    base = pix - low
    n_hi = n_pix // GROUP
    k_rows, ch = start_ref.shape
    pixels = s_ref.shape[0]
    half = pixels // 2
    step_pix = x_out.shape[-1]
    chunks = half // step_pix

    def send(src, dst, sems, device):
        return pltpu.make_async_remote_copy(
            src_ref=src, dst_ref=dst, send_sem=sems.at[0], recv_sem=sems.at[1],
            device_id=device, device_id_type=MESH,
        )

    def all_pix(f):
        def body(d, carry):
            f(d, lax.rem(pix + d, n_pix))
            return carry
        lax.fori_loop(1, n_pix, body, 0)

    loads = []
    for j in range(2 * chunks):
        part = pl.ds(j * step_pix, step_pix)
        loads.append(pltpu.make_async_copy(s_hbm.at[part], s_ref.at[part], in_sem.at[j]))
        loads[-1].start()

    barrier = pltpu.get_barrier_semaphore()
    for mate in mates:
        pl.semaphore_signal(barrier, inc=1, device_id=(pix, mate), device_id_type=MESH)
    all_pix(lambda d, to: pl.semaphore_signal(
        barrier, inc=1, device_id=(to, chan), device_id_type=MESH))
    pl.semaphore_wait(barrier, 3 + n_pix - 1)

    def swap_copy(j):
        away = pl.multiple_of(((1 - lo) * chunks + j) * step_pix, step_pix)
        return send(
            s_hbm.at[pl.ds(away, step_pix)],
            other_s.at[pl.ds(pl.multiple_of(j * step_pix, step_pix), step_pix)],
            s_sem.at[j], (pix, mates[0]))
    swap_start = send(start_ref, start_in, st_sem, (pix, mates[0]))
    swap_start.start()
    for j in range(chunks):
        swap_copy(j).start()

    total_col = jnp.zeros((8, ch), F32)
    for j in range(2 * chunks):
        loads[j].wait()
        block = s_ref[j * step_pix : (j + 1) * step_pix, :].astype(F32)
        total_col += jnp.sum(block.reshape(step_pix // 8, 8, ch), axis=0)
    col_out[...] = jnp.sum(total_col, axis=0, keepdims=True)

    def col_copy(d, to):
        return send(col_out, col_in.at[d], col_sem.at[d], (to, chan))
    all_pix(lambda d, to: col_copy(d, to).start())

    ones = jnp.ones((ch, 128), BF16)
    diagonal = lax.broadcasted_iota(jnp.int32, (128, 128), 0) == (
        lax.broadcasted_iota(jnp.int32, (128, 128), 1))
    for j in range(2 * chunks):
        sums = dot(s_ref[j * step_pix : (j + 1) * step_pix, :], ones)
        for b in range(step_pix // 128):
            square = jnp.where(diagonal, sums[b * 128 : (b + 1) * 128, :], 0.0)
            row_out[j : j + 1, b * 128 : (b + 1) * 128] = jnp.sum(
                square, axis=0, keepdims=True)
    row_copies = [
        send(row_out, row_in.at[m], row_sem.at[m], (pix, mates[m])) for m in range(3)
    ]
    for copy in row_copies:
        copy.start()

    col_in[0] = col_out[...]
    all_pix(lambda d, to: col_copy(d, to).wait())
    col_mine[...] = jnp.sum(col_in[...], axis=0)
    col_copies = [
        send(col_mine, col_chan.at[m], cc_sem.at[m], (pix, mates[m])) for m in range(3)
    ]
    for copy in col_copies:
        copy.start()
    for copy in row_copies:
        copy.wait()
    sums = (row_out[...] + row_in[0]) + (row_in[1] + row_in[2])
    for j in range(2 * chunks):
        row_sum[j] = jnp.broadcast_to(sums[j : j + 1, :], (8, step_pix))
    for copy in col_copies:
        copy.wait()
    cols = (col_mine[...] + col_chan[0]) + (col_chan[1] + col_chan[2])
    inv_total = 1.0 / jnp.sum(cols, axis=1, keepdims=True)
    shares = [col_mine[...] * inv_total, col_chan[0] * inv_total]
    share_roots = [lax.rsqrt(share) for share in shares]

    tiles = step_pix // 128

    swap_start.wait()
    load[:, :ch] = start_ref[...]
    load[:, ch:] = start_in[...]
    padded[...] = jnp.zeros_like(padded)
    rows_pad[...] = jnp.zeros_like(rows_pad)

    rows_part = k_rows // 2
    slab_lanes = ch * rows_part // (8 * GROUP)
    across = ch // slab_lanes

    def x_copy(t, h, j):
        return send(
            x_out.at[t, h, j], x_in.at[t, h, j], x_sem.at[t, h, j], (pix, mates[1]))

    def project_chunk(t, j):
        part = dot(load[...], wt[j]).astype(BF16)
        x_out[t, 0, j] = part[:rows_part]
        x_out[t, 1, j] = part[rows_part:]
        x_copy(t, 0, j).start()

    def later_half(t):
        for j in range(chunks):
            x_copy(t, 1, j).start()

    def project(t):
        def body(j, carry):
            project_chunk(t, j)
            return carry
        lax.fori_loop(0, chunks, body, 0)
        later_half(t)

    def gather(t, h, j):
        x_copy(t, h, j).wait()
        return x_out[t, h, j].astype(F32) + x_in[t, h, j].astype(F32)

    def weigh(j, q):
        i = j * tiles + q
        first = pl.multiple_of(q * 128, 128)
        line = row_sum[lo * chunks + j, 0:1, pl.ds(first, 128)]
        wide = jnp.transpose(jnp.broadcast_to(line, (128, 128)))
        wide_root = lax.rsqrt(wide)
        mine = s_ref[pl.ds(pl.multiple_of(lo * half + i * 128, 128), 128), :]
        theirs = other_s[pl.ds(pl.multiple_of(i * 128, 128), 128), :]
        for side, counts in enumerate((mine, theirs)):
            for g in range(ch // 128):
                lanes = slice(g * 128, (g + 1) * 128)
                expect = wide * shares[side][:, lanes]
                root = wide_root * share_roots[side][:, lanes]
                value = counts[:, lanes].astype(F32)
                weighted = ((value - expect) * root).astype(BF16)
                at = side * ch + g * 128
                w[j, pl.ds(first, 128), at : at + 128] = weighted
                wt[j, at : at + 128, pl.ds(first, 128)] = jnp.transpose(weighted)

    def opening(j, carry):
        swap_copy(j).wait()

        def tile(q, inner):
            weigh(j, q)
            return inner
        lax.fori_loop(0, tiles, tile, 0)
        project_chunk(0, j)
        return carry
    lax.fori_loop(0, chunks, opening, 0)
    later_half(0)

    def slab_at(i):
        return slice(8 * (i // across), 8 * (i // across) + 8), (i % across) * slab_lanes

    def accumulate(t, h, first, last):
        def body(j, carry):
            acc[...] += dot(gather(t, h, j).astype(BF16), w[j])
            return carry
        lax.fori_loop(first, last, body, 0)

    def pair_copy(t, h):
        return send(
            mate_out.at[t, h], half_in.at[t, h], half_sem.at[t, h], (pix, mates[0]))

    def pair_start(t, h):
        for i in range(GROUP):
            rows, at = slab_at(i)
            mate_out[t, h, i] = acc[rows, ch + at : ch + at + slab_lanes]
            keep[t, h, i] = acc[rows, at : at + slab_lanes]
        pair_copy(t, h).start()
        acc[...] = jnp.zeros_like(acc)

    def partner(d):
        return lax.rem(low + d, GROUP)

    def scatter_copies(t, h):
        return [
            send(keep.at[t, h, partner(d)], rs_in.at[t, h, d], rs_sem.at[t, h, d],
                 (base + partner(d), chan))
            for d in range(1, GROUP)
        ]

    def pair_finish(t, h):
        pair_copy(t, h).wait()
        keep[t, h] = keep[t, h] + half_in[t, h]
        for copy in scatter_copies(t, h):
            copy.start()

    def collect_copies(t, h):
        return [
            send(ag.at[t, h, low], ag.at[t, h, low], ag_sem.at[t, h, d],
                 (base + partner(d), chan))
            for d in range(1, GROUP)
        ]

    def scatter_finish(t, h):
        slab = keep[t, h, low]
        for d, copy in enumerate(scatter_copies(t, h), 1):
            copy.wait()
            slab = slab + rs_in[t, h, d]
        if n_hi > 1:
            hi_in[t, h, 0] = slab
            groups = [
                send(hi_in.at[t, h, 0], hi_in.at[t, h, e], hi_sem.at[t, h, e],
                     (lax.rem(pix + e * GROUP, n_pix), chan))
                for e in range(1, n_hi)
            ]
            for copy in groups:
                copy.start()
            for copy in groups:
                copy.wait()
            place = lax.div(pix, GROUP)
            slab = hi_in[t, h, lax.rem(n_hi + place, n_hi)]
            for e in range(1, n_hi):
                slab = slab + hi_in[t, h, lax.rem(n_hi + place - e, n_hi)]
        ag[t, h, low] = slab
        for copy in collect_copies(t, h):
            copy.start()

    def twin_copy(t, h):
        return send(ag.at[t, h], back_in.at[t, h], bk_sem.at[t, h], (pix, mates[0]))

    def collect_finish(t, h):
        for copy in collect_copies(t, h):
            copy.wait()
        twin_copy(t, h).start()
        for i in range(GROUP):
            rows, at = slab_at(i)
            first = k_rows + h * rows_part + rows.start
            padded[first : first + 8, at : at + slab_lanes] = ag[t, h, i]

    def iteration(t, carry):
        accumulate(t, 0, 0, chunks)
        pair_start(t, 0)
        accumulate(t, 1, 0, chunks // 2)
        pair_finish(t, 0)
        accumulate(t, 1, chunks // 2, chunks)
        pair_start(t, 1)
        scatter_finish(t, 0)
        pair_finish(t, 1)
        collect_finish(t, 0)
        scatter_finish(t, 1)
        collect_finish(t, 1)
        back = padded[k_rows : 2 * k_rows, :]
        gram_out[t] = dot(back[:rows_part], padded[k_rows:, :], NT, HIGH) + dot(
            back[rows_part:], padded[: 2 * k_rows, :], NT, HIGH)
        grams = [
            send(gram_out.at[t], gram_in.at[t, m], gram_sem.at[t, m], (pix, mates[m]))
            for m in range(3)
        ]
        for copy in grams:
            copy.start()
        split_rows(halves, back, slice(0, ch))
        for h in range(2):
            twin_copy(t, h).wait()
            for i in range(GROUP):
                rows, at = slab_at(i)
                first = h * rows_part + rows.start
                theirs[first : first + 8, at : at + slab_lanes] = back_in[t, h, i]
        split_rows(halves, theirs[...], slice(ch, 2 * ch))
        for copy in grams:
            copy.wait()
        gram = (gram_out[t] + gram_in[t, 0]) + (gram_in[t, 1] + gram_in[t, 2])
        factor = inverse_factor(jnp.concatenate([pltpu.roll(gram, 64, 1), gram], axis=0))
        load[...] = split_dot(factor, halves[...]).astype(BF16)
        project(t + 1)
        return carry
    acc[...] = jnp.zeros_like(acc)
    lax.fori_loop(0, ITERS, iteration, 0)

    n_anchor = anchors_ref.shape[0]
    order = lax.broadcasted_iota(jnp.int32, (n_anchor, step_pix), 0)
    wanted = jnp.zeros((n_anchor, step_pix), jnp.int32)
    for a in range(n_anchor):
        wanted = jnp.where(order == a, anchors_ref[a], wanted)
    wanted = wanted - pix * pixels - lo * half
    rows_half[...] = jnp.zeros_like(rows_half)

    def finish(j, carry):
        value = jnp.concatenate([gather(ITERS, 0, j), gather(ITERS, 1, j)], axis=0)
        slot = lo * chunks + j
        score[slot] = value
        send(score.at[slot], score.at[slot], sc_sem.at[j], (pix, mates[0])).start()
        positions = lax.broadcasted_iota(jnp.int32, (n_anchor, step_pix), 1)
        picks = jnp.where(positions == wanted - j * step_pix, 1.0, 0.0)
        rows_half[...] += dot(picks, value, NT, HIGH)
        return carry
    lax.fori_loop(0, chunks, finish, 0)
    pair_rows = send(rows_half, rows_half_in, rh_sem, (pix, mates[0]))
    pair_rows.start()
    pair_rows.wait()
    rows_out[...] = rows_half[...] + rows_half_in[...]

    def rows_copy(d, to):
        return send(rows_out, rows_in.at[d], rows_sem.at[d], (to, chan))
    all_pix(lambda d, to: rows_copy(d, to).start())
    rows_in[0] = rows_out[...]
    for j in range(chunks):
        slot = lo * chunks + j
        send(score.at[slot], score.at[slot], sc_sem.at[j], (pix, mates[0])).wait()
    for j in range(2 * chunks):
        part = slice(j * step_pix, (j + 1) * step_pix)
        scores_ref[:, part] = score[j]
        split_rows(pieces, score[j], part)
    all_pix(lambda d, to: rows_copy(d, to).wait())
    rows = jnp.sum(rows_in[...], axis=0)
    rows_pad[64 : 64 + n_anchor, :k_rows] = rows
    small = dot(rows_pad[64 : 64 + n_anchor, :], rows_pad[0:128, :], NT, HIGH)
    factor = inverse_factor(small)
    solved = dot(factor, rows_pad[64:192, :], precision=HIGH)
    both = dot(jnp.transpose(factor)[:n_anchor, :], solved, precision=HIGH)
    abund_ref[...] = split_dot(both, pieces[...])


def local(n_pix, spectra, start, anchors):
    pixels, ch = spectra.shape
    k = start.shape[0]
    na = anchors.shape[0]
    half = pixels // 2
    step = min(512, half)
    chunks = half // step
    n_hi = n_pix // GROUP
    vmem = pl.BlockSpec(memory_space=pltpu.VMEM)
    smem = pl.BlockSpec(memory_space=pltpu.SMEM)
    hbm = pl.BlockSpec(memory_space=pltpu.HBM)
    v = pltpu.VMEM
    sem = lambda *shape: pltpu.SemaphoreType.DMA(tuple(shape) + (2,))
    slabs = lambda count: v((ITERS, 2, count, 8, ch * (k // 2) // (8 * GROUP)), F32)
    scratch = [
        v((pixels, ch), BF16), v((half, ch), BF16), v((k, ch), BF16), v((1, ch), F32),
        v((n_pix, 1, ch), F32), v((1, ch), F32), v((3, 1, ch), F32), v((2 * chunks, step), F32),
        v((3, 2 * chunks, step), F32), v((2 * chunks, 8, step), F32),
        v((chunks, step, 2 * ch), BF16), v((chunks, 2 * ch, step), BF16), v((k, 2 * ch), BF16),
        v((ITERS + 1, 2, chunks, k // 2, step), BF16),
        v((ITERS + 1, 2, chunks, k // 2, step), BF16),
        v((k // 2, 2 * ch), F32), slabs(GROUP), slabs(GROUP), slabs(GROUP), slabs(GROUP),
        slabs(n_hi), slabs(GROUP), slabs(GROUP), v((3 * k, ch), F32),
        v((ITERS, k // 2, 2 * k), F32), v((ITERS, 3, k // 2, 2 * k), F32),
        v((2 * chunks, k, step), F32), v((na, k), F32), v((na, k), F32), v((na, k), F32),
        v((n_pix, na, k), F32), v((192, 128), F32),
        v((2 * k, 2 * ch), BF16), v((k, ch), F32), v((2 * k, pixels), BF16),
        pltpu.SemaphoreType.DMA((2 * chunks,)), sem(chunks), sem(), sem(n_pix), sem(3), sem(3), sem(ITERS + 1, 2, chunks),
        sem(ITERS, 2), sem(ITERS, 2, GROUP), sem(ITERS, 2, n_hi), sem(ITERS, 2, GROUP),
        sem(ITERS, 2), sem(ITERS, 3),
        sem(chunks), sem(), sem(n_pix),
    ]
    return pl.pallas_call(
        functools.partial(kernel, n_pix),
        out_shape=(
            jax.ShapeDtypeStruct((k, pixels), F32),
            jax.ShapeDtypeStruct((na, pixels), F32),
        ),
        in_specs=[hbm, vmem, smem],
        out_specs=(vmem, vmem),
        scratch_shapes=scratch,
        compiler_params=pltpu.CompilerParams(
            collective_id=0, has_side_effects=True, vmem_limit_bytes=36 * 1024 * 1024
        ),
    )(spectra, start, anchors)


def solution(mesh):
    placed = (P("pix", "chan"), P(None, "chan"), P())
    return jax.shard_map(
        functools.partial(local, mesh.shape["pix"]),
        mesh=mesh,
        in_specs=placed,
        out_specs=(P(None, "pix"), P(None, "pix")),
        check_vma=False,
    )
```

```python
import functools

import jax
import jax.numpy as jnp
from jax import lax
from jax.experimental import pallas as pl
from jax.experimental.pallas import tpu as pltpu
from jax.sharding import PartitionSpec as P

ITERS = 5
FIRST_LATE = 2
GROUP = 8
MESH = pl.DeviceIdType.MESH
HIGH = lax.Precision.HIGHEST
F32 = jnp.float32
BF16 = jnp.bfloat16
NT = (((1,), (1,)), ((), ()))


def dot(a, b, dims=(((1,), (0,)), ((), ())), precision=None):
    return lax.dot_general(a, b, dims, precision=precision, preferred_element_type=F32)


def inverse_factor(gram):
    n = gram.shape[0]
    rows = lax.broadcasted_iota(jnp.int32, (n, 128), 0)
    lanes = lax.broadcasted_iota(jnp.int32, (n, 128), 1)
    full = jnp.where(lanes < 64, jnp.where(lanes == rows, 1.0, 0.0), gram)
    sub = lax.broadcasted_iota(jnp.int32, (8, 128), 0)
    count = n // 8
    blocks = [full[8 * i : 8 * i + 8, :] for i in range(count)]
    done = []
    for home in range(count):
        spread = [
            [jnp.broadcast_to(block[:, at : at + 1], (8, 128))
             for at in range(64 + 8 * home, 72 + 8 * home)]
            for block in blocks
        ]
        pivots = jnp.ones((8, 128), F32)
        for r in range(8):
            inverse = 1.0 / spread[0][r][r : r + 1, :]
            pivots = jnp.where(sub == r, spread[0][r], pivots)
            line = blocks[0][r : r + 1, :] * inverse
            later = {c: spread[0][c][r : r + 1, :] * inverse for c in range(r + 1, 8)}
            for i in range(len(blocks)):
                ratio = spread[i][r]
                if i == 0:
                    ratio = jnp.where(sub > r, ratio, 0.0)
                for c, value in later.items():
                    spread[i][c] = spread[i][c] - ratio * value
                blocks[i] = blocks[i] - ratio * line
        done.append(blocks[0] * lax.rsqrt(pivots))
        blocks = blocks[1:]
    return jnp.where(lanes < 64, jnp.concatenate(done, axis=0), 0.0)


def split_rows(ref, value, lanes):
    top = value.astype(BF16)
    n = value.shape[0]
    ref[:n, lanes] = top
    ref[n:, lanes] = (value - top.astype(F32)).astype(BF16)


def split_dot(left, pair):
    top = left.astype(BF16)
    low = (left - top.astype(F32)).astype(BF16)
    twice = (top.astype(F32) + pltpu.roll(top.astype(F32), 64, 1)).astype(BF16)
    n = left.shape[0]
    out = dot(jnp.concatenate([twice, low], axis=0), pair)
    return out[:n] + out[n:]


def kernel(
    n_pix, s_hbm, start_ref, anchors_ref, scores_ref, abund_ref,
    s_ref, other_s, start_in, col_out, col_in, col_mine, col_chan, row_out, row_in, row_sum,
    w, wt, load, x_out, x_in, acc, half_in, keep, rs_in, hi_in, ag, back_in, padded,
    gram_out, gram_in, score, rows_half, rows_half_in, rows_out, rows_in, rows_pad,
    halves, shares_split, factor_ref, pieces, in_sem, s_sem, st_sem, col_sem, cc_sem, row_sem, x_sem, half_sem, rs_sem, hi_sem, ag_sem,
    bk_sem, gram_sem, sc_sem, rh_sem, rows_sem,
):
    pix = lax.axis_index("pix")
    chan = lax.axis_index("chan")
    lo, hi = lax.rem(chan, 2), lax.div(chan, 2)
    mates = [hi * 2 + 1 - lo, (1 - hi) * 2 + lo, (1 - hi) * 2 + 1 - lo]
    low = lax.rem(pix, GROUP)
    base = pix - low
    n_hi = n_pix // GROUP
    k_rows, ch = start_ref.shape
    pixels = s_ref.shape[0]
    half = pixels // 2
    step_pix = x_out.shape[-1]
    chunks = half // step_pix

    def send(src, dst, sems, device):
        return pltpu.make_async_remote_copy(
            src_ref=src, dst_ref=dst, send_sem=sems.at[0], recv_sem=sems.at[1],
            device_id=device, device_id_type=MESH,
        )

    def all_pix(f):
        def body(d, carry):
            f(d, lax.rem(pix + d, n_pix))
            return carry
        lax.fori_loop(1, n_pix, body, 0)

    loads = []
    for j in range(2 * chunks):
        part = pl.ds(j * step_pix, step_pix)
        loads.append(pltpu.make_async_copy(s_hbm.at[part], s_ref.at[part], in_sem.at[j]))
        loads[-1].start()

    barrier = pltpu.get_barrier_semaphore()
    for mate in mates:
        pl.semaphore_signal(barrier, inc=1, device_id=(pix, mate), device_id_type=MESH)
    all_pix(lambda d, to: pl.semaphore_signal(
        barrier, inc=1, device_id=(to, chan), device_id_type=MESH))
    pl.semaphore_wait(barrier, 3 + n_pix - 1)

    def swap_copy(j):
        away = pl.multiple_of(((1 - lo) * chunks + j) * step_pix, step_pix)
        return send(
            s_hbm.at[pl.ds(away, step_pix)],
            other_s.at[pl.ds(pl.multiple_of(j * step_pix, step_pix), step_pix)],
            s_sem.at[j], (pix, mates[0]))
    swap_start = send(start_ref, start_in, st_sem, (pix, mates[0]))
    swap_start.start()
    for j in range(chunks):
        swap_copy(j).start()

    total_col = jnp.zeros((8, ch), F32)
    for j in range(2 * chunks):
        loads[j].wait()
        block = s_ref[j * step_pix : (j + 1) * step_pix, :].astype(F32)
        total_col += jnp.sum(block.reshape(step_pix // 8, 8, ch), axis=0)
    col_out[...] = jnp.sum(total_col, axis=0, keepdims=True)

    def col_copy(d, to):
        return send(col_out, col_in.at[d], col_sem.at[d], (to, chan))
    all_pix(lambda d, to: col_copy(d, to).start())

    ones = jnp.ones((ch, 128), BF16)
    diagonal = lax.broadcasted_iota(jnp.int32, (128, 128), 0) == (
        lax.broadcasted_iota(jnp.int32, (128, 128), 1))
    for j in range(2 * chunks):
        sums = dot(s_ref[j * step_pix : (j + 1) * step_pix, :], ones)
        for b in range(step_pix // 128):
            square = jnp.where(diagonal, sums[b * 128 : (b + 1) * 128, :], 0.0)
            row_out[j : j + 1, b * 128 : (b + 1) * 128] = jnp.sum(
                square, axis=0, keepdims=True)
    row_copies = [
        send(row_out, row_in.at[m], row_sem.at[m], (pix, mates[m])) for m in range(3)
    ]
    for copy in row_copies:
        copy.start()

    col_in[0] = col_out[...]
    all_pix(lambda d, to: col_copy(d, to).wait())
    col_mine[...] = jnp.sum(col_in[...], axis=0)
    col_copies = [
        send(col_mine, col_chan.at[m], cc_sem.at[m], (pix, mates[m])) for m in range(3)
    ]
    for copy in col_copies:
        copy.start()
    for copy in row_copies:
        copy.wait()
    sums = (row_out[...] + row_in[0]) + (row_in[1] + row_in[2])
    for j in range(2 * chunks):
        row_sum[j] = jnp.broadcast_to(sums[j : j + 1, :], (8, step_pix))
    for copy in col_copies:
        copy.wait()
    cols = (col_mine[...] + col_chan[0]) + (col_chan[1] + col_chan[2])
    inv_total = 1.0 / jnp.sum(cols, axis=1, keepdims=True)
    shares = [col_mine[...] * inv_total, col_chan[0] * inv_total]
    share_roots = [lax.rsqrt(share) for share in shares]

    tiles = step_pix // 128

    swap_start.wait()
    load[:, :ch] = start_ref[...]
    load[:, ch:] = start_in[...]
    padded[...] = jnp.zeros_like(padded)
    rows_pad[...] = jnp.zeros_like(rows_pad)

    def x_copy(t, j):
        return send(x_out.at[t, j], x_in.at[t, j], x_sem.at[t, j], (pix, mates[1]))

    def project_chunk(t, j):
        x_out[t, j] = dot(load[...], wt[j]).astype(BF16)
        x_copy(t, j).start()

    def project(t):
        def body(j, carry):
            project_chunk(t, j)
            return carry
        lax.fori_loop(0, chunks, body, 0)

    def gather(t, j):
        x_copy(t, j).wait()
        return x_out[t, j].astype(F32) + x_in[t, j].astype(F32)

    def normal(value):
        split_rows(shares_split, value, slice(0, step_pix))
        return split_dot(factor_ref[...], shares_split[...])

    def weigh(j, q):
        i = j * tiles + q
        first = pl.multiple_of(q * 128, 128)
        line = row_sum[lo * chunks + j, 0:1, pl.ds(first, 128)]
        wide = jnp.transpose(jnp.broadcast_to(line, (128, 128)))
        wide_root = lax.rsqrt(wide)
        mine = s_ref[pl.ds(pl.multiple_of(lo * half + i * 128, 128), 128), :]
        theirs = other_s[pl.ds(pl.multiple_of(i * 128, 128), 128), :]
        for side, counts in enumerate((mine, theirs)):
            for g in range(ch // 128):
                lanes = slice(g * 128, (g + 1) * 128)
                expect = wide * shares[side][:, lanes]
                root = wide_root * share_roots[side][:, lanes]
                value = counts[:, lanes].astype(F32)
                weighted = ((value - expect) * root).astype(BF16)
                at = side * ch + g * 128
                w[j, pl.ds(first, 128), at : at + 128] = weighted
                wt[j, at : at + 128, pl.ds(first, 128)] = jnp.transpose(weighted)

    def opening(j, carry):
        swap_copy(j).wait()

        def tile(q, inner):
            weigh(j, q)
            return inner
        lax.fori_loop(0, tiles, tile, 0)
        project_chunk(0, j)
        return carry
    lax.fori_loop(0, chunks, opening, 0)

    per = k_rows // GROUP

    def iteration(late, defer, t, carry):
        acc[...] = jnp.zeros_like(acc)

        def body(j, carry):
            value = gather(t, j)
            if late:
                value = normal(value)
            acc[...] += dot(value.astype(BF16), w[j])
            return carry
        lax.fori_loop(0, chunks, body, 0)

        keep[t, 0] = acc[:, ch:]
        copy = send(keep.at[t, 0], half_in.at[t], half_sem.at[t], (pix, mates[0]))
        copy.start()
        copy.wait()
        keep[t, 1] = acc[:, :ch] + half_in[t]

        def partner(d):
            return lax.rem(low + d, GROUP)
        spread = [
            send(
                keep.at[t, 1, pl.ds(pl.multiple_of(partner(d) * per, per), per)],
                rs_in.at[t, d], rs_sem.at[t, d], (base + partner(d), chan))
            for d in range(1, GROUP)
        ]
        for copy in spread:
            copy.start()
        slab = keep[t, 1, pl.ds(pl.multiple_of(low * per, per), per), :]
        for d, copy in enumerate(spread, 1):
            copy.wait()
            slab = slab + rs_in[t, d]
        if n_hi > 1:
            hi_in[t, 0] = slab
            across = [
                send(hi_in.at[t, 0], hi_in.at[t, e], hi_sem.at[t, e],
                     (lax.rem(pix + e * GROUP, n_pix), chan))
                for e in range(1, n_hi)
            ]
            for copy in across:
                copy.start()
            for copy in across:
                copy.wait()
            slab = hi_in[t, lax.rem(n_hi + lax.div(pix, GROUP), n_hi)]
            for e in range(1, n_hi):
                slab = slab + hi_in[t, lax.rem(n_hi + lax.div(pix, GROUP) - e, n_hi)]
        mine = pl.ds(pl.multiple_of(low * per, per), per)
        ag[t, mine] = slab
        collect = [
            send(ag.at[t, mine], ag.at[t, mine], ag_sem.at[t, d], (base + partner(d), chan))
            for d in range(1, GROUP)
        ]
        for copy in collect:
            copy.start()
        for copy in collect:
            copy.wait()
        twin = send(ag.at[t], back_in.at[t], bk_sem.at[t], (pix, mates[0]))
        twin.start()
        back = ag[t]
        padded[k_rows : 2 * k_rows, :] = back
        gram_out[t] = dot(back[: k_rows // 2], padded[k_rows:, :], NT, HIGH) + dot(
            back[k_rows // 2 :], padded[: 2 * k_rows, :], NT, HIGH)
        grams = [
            send(gram_out.at[t], gram_in.at[t, m], gram_sem.at[t, m], (pix, mates[m]))
            for m in range(3)
        ]
        for copy in grams:
            copy.start()
        def factor_of():
            for copy in grams:
                copy.wait()
            gram = (gram_out[t] + gram_in[t, 0]) + (gram_in[t, 1] + gram_in[t, 2])
            return inverse_factor(
                jnp.concatenate([pltpu.roll(gram, 64, 1), gram], axis=0))

        if defer:
            load[:, :ch] = back.astype(BF16)
            twin.wait()
            load[:, ch:] = back_in[t].astype(BF16)
            project(t + 1)
            factor_ref[...] = factor_of()
        else:
            split_rows(halves, back, slice(0, ch))
            factor = factor_of()
            twin.wait()
            split_rows(halves, back_in[t], slice(ch, 2 * ch))
            load[...] = split_dot(factor, halves[...]).astype(BF16)
            project(t + 1)
        return carry
    plain = functools.partial(iteration, False, False)
    first = functools.partial(iteration, False, True)
    later = functools.partial(iteration, True, True)
    lax.fori_loop(0, FIRST_LATE, plain, 0)
    first(FIRST_LATE, 0)
    lax.fori_loop(FIRST_LATE + 1, ITERS, later, 0)

    n_anchor = anchors_ref.shape[0]
    order = lax.broadcasted_iota(jnp.int32, (n_anchor, step_pix), 0)
    wanted = jnp.zeros((n_anchor, step_pix), jnp.int32)
    for a in range(n_anchor):
        wanted = jnp.where(order == a, anchors_ref[a], wanted)
    wanted = wanted - pix * pixels - lo * half
    rows_half[...] = jnp.zeros_like(rows_half)

    def finish(j, carry):
        value = normal(gather(ITERS, j))
        slot = lo * chunks + j
        score[slot] = value
        send(score.at[slot], score.at[slot], sc_sem.at[j], (pix, mates[0])).start()
        positions = lax.broadcasted_iota(jnp.int32, (n_anchor, step_pix), 1)
        picks = jnp.where(positions == wanted - j * step_pix, 1.0, 0.0)
        rows_half[...] += dot(picks, value, NT, HIGH)
        return carry
    lax.fori_loop(0, chunks, finish, 0)
    pair_rows = send(rows_half, rows_half_in, rh_sem, (pix, mates[0]))
    pair_rows.start()
    pair_rows.wait()
    rows_out[...] = rows_half[...] + rows_half_in[...]

    def rows_copy(d, to):
        return send(rows_out, rows_in.at[d], rows_sem.at[d], (to, chan))
    all_pix(lambda d, to: rows_copy(d, to).start())
    rows_in[0] = rows_out[...]
    for j in range(chunks):
        slot = lo * chunks + j
        send(score.at[slot], score.at[slot], sc_sem.at[j], (pix, mates[0])).wait()
    for j in range(2 * chunks):
        part = slice(j * step_pix, (j + 1) * step_pix)
        scores_ref[:, part] = score[j]
        split_rows(pieces, score[j], part)
    all_pix(lambda d, to: rows_copy(d, to).wait())
    rows = jnp.sum(rows_in[...], axis=0)
    rows_pad[64 : 64 + n_anchor, :k_rows] = rows
    small = dot(rows_pad[64 : 64 + n_anchor, :], rows_pad[0:128, :], NT, HIGH)
    factor = inverse_factor(small)
    solved = dot(factor, rows_pad[64:192, :], precision=HIGH)
    both = dot(jnp.transpose(factor)[:n_anchor, :], solved, precision=HIGH)
    abund_ref[...] = split_dot(both, pieces[...])


def local(n_pix, spectra, start, anchors):
    pixels, ch = spectra.shape
    k = start.shape[0]
    na = anchors.shape[0]
    half = pixels // 2
    step = min(512, half)
    chunks = half // step
    n_hi = n_pix // GROUP
    vmem = pl.BlockSpec(memory_space=pltpu.VMEM)
    smem = pl.BlockSpec(memory_space=pltpu.SMEM)
    hbm = pl.BlockSpec(memory_space=pltpu.HBM)
    v = pltpu.VMEM
    sem = lambda *shape: pltpu.SemaphoreType.DMA(tuple(shape) + (2,))
    scratch = [
        v((pixels, ch), BF16), v((half, ch), BF16), v((k, ch), BF16), v((1, ch), F32),
        v((n_pix, 1, ch), F32), v((1, ch), F32), v((3, 1, ch), F32), v((2 * chunks, step), F32),
        v((3, 2 * chunks, step), F32), v((2 * chunks, 8, step), F32),
        v((chunks, step, 2 * ch), BF16), v((chunks, 2 * ch, step), BF16), v((k, 2 * ch), BF16),
        v((ITERS + 1, chunks, k, step), BF16), v((ITERS + 1, chunks, k, step), BF16),
        v((k, 2 * ch), F32), v((ITERS, k, ch), F32), v((ITERS, 2, k, ch), F32),
        v((ITERS, GROUP, k // GROUP, ch), F32), v((ITERS, n_hi, k // GROUP, ch), F32),
        v((ITERS, k, ch), F32), v((ITERS, k, ch), F32), v((3 * k, ch), F32),
        v((ITERS, k // 2, 2 * k), F32), v((ITERS, 3, k // 2, 2 * k), F32),
        v((2 * chunks, k, step), F32), v((na, k), F32), v((na, k), F32), v((na, k), F32),
        v((n_pix, na, k), F32), v((192, 128), F32),
        v((2 * k, 2 * ch), BF16), v((2 * k, step), BF16), v((k, 128), F32),
        v((2 * k, pixels), BF16),
        pltpu.SemaphoreType.DMA((2 * chunks,)), sem(chunks), sem(), sem(n_pix), sem(3), sem(3), sem(ITERS + 1, chunks), sem(ITERS),
        sem(ITERS, GROUP), sem(ITERS, n_hi), sem(ITERS, GROUP), sem(ITERS), sem(ITERS, 3),
        sem(chunks), sem(), sem(n_pix),
    ]
    return pl.pallas_call(
        functools.partial(kernel, n_pix),
        out_shape=(
            jax.ShapeDtypeStruct((k, pixels), F32),
            jax.ShapeDtypeStruct((na, pixels), F32),
        ),
        in_specs=[hbm, vmem, smem],
        out_specs=(vmem, vmem),
        scratch_shapes=scratch,
        compiler_params=pltpu.CompilerParams(
            collective_id=0, has_side_effects=True, vmem_limit_bytes=58 * 1024 * 1024
        ),
    )(spectra, start, anchors)


def solution(mesh):
    placed = (P("pix", "chan"), P(None, "chan"), P())
    return jax.shard_map(
        functools.partial(local, mesh.shape["pix"]),
        mesh=mesh,
        in_specs=placed,
        out_specs=(P(None, "pix"), P(None, "pix")),
        check_vma=False,
    )
```

```python
import functools

import jax
import jax.numpy as jnp
from jax import lax
from jax.experimental import pallas as pl
from jax.experimental.pallas import tpu as pltpu
from jax.sharding import PartitionSpec as P

ITERS = 5
FIRST_LATE = 2
GROUP = 8
MESH = pl.DeviceIdType.MESH
HIGH = lax.Precision.HIGHEST
F32 = jnp.float32
BF16 = jnp.bfloat16
NT = (((1,), (1,)), ((), ()))


def dot(a, b, dims=(((1,), (0,)), ((), ())), precision=None):
    return lax.dot_general(a, b, dims, precision=precision, preferred_element_type=F32)


def inverse_factor(gram):
    n = gram.shape[0]
    rows = lax.broadcasted_iota(jnp.int32, (n, 128), 0)
    lanes = lax.broadcasted_iota(jnp.int32, (n, 128), 1)
    full = jnp.where(lanes < 64, jnp.where(lanes == rows, 1.0, 0.0), gram)
    sub = lax.broadcasted_iota(jnp.int32, (8, 128), 0)
    count = n // 8
    blocks = [full[8 * i : 8 * i + 8, :] for i in range(count)]
    done = []
    for home in range(count):
        spread = [
            [jnp.broadcast_to(block[:, at : at + 1], (8, 128))
             for at in range(64 + 8 * home, 72 + 8 * home)]
            for block in blocks
        ]
        pivots = jnp.ones((8, 128), F32)
        for r in range(8):
            inverse = 1.0 / spread[0][r][r : r + 1, :]
            pivots = jnp.where(sub == r, spread[0][r], pivots)
            line = blocks[0][r : r + 1, :] * inverse
            later = {c: spread[0][c][r : r + 1, :] * inverse for c in range(r + 1, 8)}
            for i in range(len(blocks)):
                ratio = spread[i][r]
                if i == 0:
                    ratio = jnp.where(sub > r, ratio, 0.0)
                for c, value in later.items():
                    spread[i][c] = spread[i][c] - ratio * value
                blocks[i] = blocks[i] - ratio * line
        done.append(blocks[0] * lax.rsqrt(pivots))
        blocks = blocks[1:]
    return jnp.where(lanes < 64, jnp.concatenate(done, axis=0), 0.0)


def split_rows(ref, value, lanes):
    top = value.astype(BF16)
    n = value.shape[0]
    ref[:n, lanes] = top
    ref[n:, lanes] = (value - top.astype(F32)).astype(BF16)


def split_dot(left, pair):
    top = left.astype(BF16)
    low = (left - top.astype(F32)).astype(BF16)
    twice = (top.astype(F32) + pltpu.roll(top.astype(F32), 64, 1)).astype(BF16)
    n = left.shape[0]
    out = dot(jnp.concatenate([twice, low], axis=0), pair)
    return out[:n] + out[n:]


def kernel(
    n_pix, s_hbm, start_ref, anchors_ref, scores_ref, abund_ref,
    s_ref, other_s, start_in, col_out, col_in, col_mine, col_chan, row_out, row_in, row_sum,
    w, wt, load, x_out, x_in, acc, half_in, keep, rs_in, hi_in, ag, back_in, padded,
    gram_out, gram_in, score, rows_half, rows_half_in, rows_out, rows_in, rows_pad,
    halves, shares_split, factor_ref, pieces,
    keep16, rs16, hi16, ag16, back16_in, pad16, in_sem, s_sem, st_sem, col_sem, cc_sem, row_sem, x_sem, half_sem, rs_sem, hi_sem, ag_sem,
    bk_sem, gram_sem, sc_sem, rh_sem, rows_sem,
):
    pix = lax.axis_index("pix")
    chan = lax.axis_index("chan")
    lo, hi = lax.rem(chan, 2), lax.div(chan, 2)
    mates = [hi * 2 + 1 - lo, (1 - hi) * 2 + lo, (1 - hi) * 2 + 1 - lo]
    low = lax.rem(pix, GROUP)
    base = pix - low
    n_hi = n_pix // GROUP
    k_rows, ch = start_ref.shape
    pixels = s_ref.shape[0]
    half = pixels // 2
    step_pix = x_out.shape[-1]
    chunks = half // step_pix

    def send(src, dst, sems, device):
        return pltpu.make_async_remote_copy(
            src_ref=src, dst_ref=dst, send_sem=sems.at[0], recv_sem=sems.at[1],
            device_id=device, device_id_type=MESH,
        )

    def all_pix(f):
        def body(d, carry):
            f(d, lax.rem(pix + d, n_pix))
            return carry
        lax.fori_loop(1, n_pix, body, 0)

    loads = []
    for j in range(2 * chunks):
        part = pl.ds(j * step_pix, step_pix)
        loads.append(pltpu.make_async_copy(s_hbm.at[part], s_ref.at[part], in_sem.at[j]))
        loads[-1].start()

    barrier = pltpu.get_barrier_semaphore()
    for mate in mates:
        pl.semaphore_signal(barrier, inc=1, device_id=(pix, mate), device_id_type=MESH)
    all_pix(lambda d, to: pl.semaphore_signal(
        barrier, inc=1, device_id=(to, chan), device_id_type=MESH))
    pl.semaphore_wait(barrier, 3 + n_pix - 1)

    def swap_copy(j):
        away = pl.multiple_of(((1 - lo) * chunks + j) * step_pix, step_pix)
        return send(
            s_hbm.at[pl.ds(away, step_pix)],
            other_s.at[pl.ds(pl.multiple_of(j * step_pix, step_pix), step_pix)],
            s_sem.at[j], (pix, mates[0]))
    swap_start = send(start_ref, start_in, st_sem, (pix, mates[0]))
    swap_start.start()
    for j in range(chunks):
        swap_copy(j).start()

    total_col = jnp.zeros((8, ch), F32)
    for j in range(2 * chunks):
        loads[j].wait()
        block = s_ref[j * step_pix : (j + 1) * step_pix, :].astype(F32)
        total_col += jnp.sum(block.reshape(step_pix // 8, 8, ch), axis=0)
    col_out[...] = jnp.sum(total_col, axis=0, keepdims=True)

    def col_copy(d, to):
        return send(col_out, col_in.at[d], col_sem.at[d], (to, chan))
    all_pix(lambda d, to: col_copy(d, to).start())

    ones = jnp.ones((ch, 128), BF16)
    diagonal = lax.broadcasted_iota(jnp.int32, (128, 128), 0) == (
        lax.broadcasted_iota(jnp.int32, (128, 128), 1))
    for j in range(2 * chunks):
        sums = dot(s_ref[j * step_pix : (j + 1) * step_pix, :], ones)
        for b in range(step_pix // 128):
            square = jnp.where(diagonal, sums[b * 128 : (b + 1) * 128, :], 0.0)
            row_out[j : j + 1, b * 128 : (b + 1) * 128] = jnp.sum(
                square, axis=0, keepdims=True)
    row_copies = [
        send(row_out, row_in.at[m], row_sem.at[m], (pix, mates[m])) for m in range(3)
    ]
    for copy in row_copies:
        copy.start()

    col_in[0] = col_out[...]
    all_pix(lambda d, to: col_copy(d, to).wait())
    col_mine[...] = jnp.sum(col_in[...], axis=0)
    col_copies = [
        send(col_mine, col_chan.at[m], cc_sem.at[m], (pix, mates[m])) for m in range(3)
    ]
    for copy in col_copies:
        copy.start()
    for copy in row_copies:
        copy.wait()
    sums = (row_out[...] + row_in[0]) + (row_in[1] + row_in[2])
    for j in range(2 * chunks):
        row_sum[j] = jnp.broadcast_to(sums[j : j + 1, :], (8, step_pix))
    for copy in col_copies:
        copy.wait()
    cols = (col_mine[...] + col_chan[0]) + (col_chan[1] + col_chan[2])
    inv_total = 1.0 / jnp.sum(cols, axis=1, keepdims=True)
    shares = [col_mine[...] * inv_total, col_chan[0] * inv_total]
    share_roots = [lax.rsqrt(share) for share in shares]

    tiles = step_pix // 128

    swap_start.wait()
    load[:, :ch] = start_ref[...]
    load[:, ch:] = start_in[...]
    padded[...] = jnp.zeros_like(padded)
    pad16[...] = jnp.zeros_like(pad16)
    rows_pad[...] = jnp.zeros_like(rows_pad)

    def x_copy(t, j):
        return send(x_out.at[t, j], x_in.at[t, j], x_sem.at[t, j], (pix, mates[1]))

    def project_chunk(t, j):
        x_out[t, j] = dot(load[...], wt[j]).astype(BF16)
        x_copy(t, j).start()

    def project(t):
        def body(j, carry):
            project_chunk(t, j)
            return carry
        lax.fori_loop(0, chunks, body, 0)

    def gather(t, j):
        x_copy(t, j).wait()
        return x_out[t, j].astype(F32) + x_in[t, j].astype(F32)

    def normal(value):
        split_rows(shares_split, value, slice(0, step_pix))
        return split_dot(factor_ref[...], shares_split[...])

    def weigh(j, q):
        i = j * tiles + q
        first = pl.multiple_of(q * 128, 128)
        line = row_sum[lo * chunks + j, 0:1, pl.ds(first, 128)]
        wide = jnp.transpose(jnp.broadcast_to(line, (128, 128)))
        wide_root = lax.rsqrt(wide)
        mine = s_ref[pl.ds(pl.multiple_of(lo * half + i * 128, 128), 128), :]
        theirs = other_s[pl.ds(pl.multiple_of(i * 128, 128), 128), :]
        for side, counts in enumerate((mine, theirs)):
            for g in range(ch // 128):
                lanes = slice(g * 128, (g + 1) * 128)
                expect = wide * shares[side][:, lanes]
                root = wide_root * share_roots[side][:, lanes]
                value = counts[:, lanes].astype(F32)
                weighted = ((value - expect) * root).astype(BF16)
                at = side * ch + g * 128
                w[j, pl.ds(first, 128), at : at + 128] = weighted
                wt[j, at : at + 128, pl.ds(first, 128)] = jnp.transpose(weighted)

    def opening(j, carry):
        swap_copy(j).wait()

        def tile(q, inner):
            weigh(j, q)
            return inner
        lax.fori_loop(0, tiles, tile, 0)
        project_chunk(0, j)
        return carry
    lax.fori_loop(0, chunks, opening, 0)

    per = k_rows // GROUP

    def iteration(late, defer, t, carry):
        acc[...] = jnp.zeros_like(acc)

        def body(j, carry):
            value = gather(t, j)
            if late:
                value = normal(value)
            acc[...] += dot(value.astype(BF16), w[j])
            return carry
        lax.fori_loop(0, chunks, body, 0)

        keep[t, 0] = acc[:, ch:]
        copy = send(keep.at[t, 0], half_in.at[t], half_sem.at[t], (pix, mates[0]))
        copy.start()
        copy.wait()
        if defer:
            narrow(t)
        else:
            wide_sums(t)
        return carry

    def partner(d):
        return lax.rem(low + d, GROUP)

    def across_groups(t, slab, buffer):
        if n_hi == 1:
            return slab
        buffer[t, 0] = slab
        across = [
            send(buffer.at[t, 0], buffer.at[t, e], hi_sem.at[t, e],
                 (lax.rem(pix + e * GROUP, n_pix), chan))
            for e in range(1, n_hi)
        ]
        for copy in across:
            copy.start()
        for copy in across:
            copy.wait()
        place = lax.div(pix, GROUP)
        slab = buffer[t, lax.rem(n_hi + place, n_hi)]
        for e in range(1, n_hi):
            slab = slab + buffer[t, lax.rem(n_hi + place - e, n_hi)]
        return slab

    def gram_copies(t):
        return [
            send(gram_out.at[t], gram_in.at[t, m], gram_sem.at[t, m], (pix, mates[m]))
            for m in range(3)
        ]

    def factor_of(t):
        for copy in gram_copies(t):
            copy.wait()
        gram = (gram_out[t] + gram_in[t, 0]) + (gram_in[t, 1] + gram_in[t, 2])
        return inverse_factor(
            jnp.concatenate([pltpu.roll(gram, 64, 1), gram], axis=0))

    slab_lanes = ch * k_rows // (16 * GROUP)
    per_line = ch // slab_lanes

    def slab_at(i):
        return 16 * (i // per_line), (i % per_line) * slab_lanes

    def narrow(t):
        for i in range(GROUP):
            r, c = slab_at(i)
            part = acc[r : r + 16, c : c + slab_lanes]
            part = part + half_in[t, r : r + 16, c : c + slab_lanes]
            keep16[t, i] = part.astype(BF16)
        spread = [
            send(keep16.at[t, partner(d)], rs16.at[t, d], rs_sem.at[t, d],
                 (base + partner(d), chan))
            for d in range(1, GROUP)
        ]
        for copy in spread:
            copy.start()
        slab = keep16[t, low].astype(F32)
        for d, copy in enumerate(spread, 1):
            copy.wait()
            slab = slab + rs16[t, d].astype(F32)
        slab = across_groups(t, slab, hi16)
        ag16[t, low] = slab.astype(BF16)
        collect = [
            send(ag16.at[t, low], ag16.at[t, low], ag_sem.at[t, d], (base + partner(d), chan))
            for d in range(1, GROUP)
        ]
        for copy in collect:
            copy.start()
        for copy in collect:
            copy.wait()
        twin = send(ag16.at[t], back16_in.at[t], bk_sem.at[t], (pix, mates[0]))
        twin.start()
        for i in range(GROUP):
            r, c = slab_at(i)
            load[r : r + 16, c : c + slab_lanes] = ag16[t, i]
            pad16[k_rows + r : k_rows + r + 16, c : c + slab_lanes] = ag16[t, i]
        gram_out[t] = dot(load[: k_rows // 2, :ch], pad16[k_rows:, :], NT) + dot(
            load[k_rows // 2 :, :ch], pad16[: 2 * k_rows, :], NT)
        for copy in gram_copies(t):
            copy.start()
        twin.wait()
        for i in range(GROUP):
            r, c = slab_at(i)
            load[r : r + 16, ch + c : ch + c + slab_lanes] = back16_in[t, i]
        project(t + 1)
        factor_ref[...] = factor_of(t)

    def wide_sums(t):
        keep[t, 1] = acc[:, :ch] + half_in[t]
        spread = [
            send(
                keep.at[t, 1, pl.ds(pl.multiple_of(partner(d) * per, per), per)],
                rs_in.at[t, d], rs_sem.at[t, d], (base + partner(d), chan))
            for d in range(1, GROUP)
        ]
        for copy in spread:
            copy.start()
        slab = keep[t, 1, pl.ds(pl.multiple_of(low * per, per), per), :]
        for d, copy in enumerate(spread, 1):
            copy.wait()
            slab = slab + rs_in[t, d]
        slab = across_groups(t, slab, hi_in)
        mine = pl.ds(pl.multiple_of(low * per, per), per)
        ag[t, mine] = slab
        collect = [
            send(ag.at[t, mine], ag.at[t, mine], ag_sem.at[t, d], (base + partner(d), chan))
            for d in range(1, GROUP)
        ]
        for copy in collect:
            copy.start()
        for copy in collect:
            copy.wait()
        twin = send(ag.at[t], back_in.at[t], bk_sem.at[t], (pix, mates[0]))
        twin.start()
        back = ag[t]
        padded[k_rows : 2 * k_rows, :] = back
        gram_out[t] = dot(back[: k_rows // 2], padded[k_rows:, :], NT, HIGH) + dot(
            back[k_rows // 2 :], padded[: 2 * k_rows, :], NT, HIGH)
        for copy in gram_copies(t):
            copy.start()
        split_rows(halves, back, slice(0, ch))
        factor = factor_of(t)
        twin.wait()
        split_rows(halves, back_in[t], slice(ch, 2 * ch))
        load[...] = split_dot(factor, halves[...]).astype(BF16)
        project(t + 1)

    plain = functools.partial(iteration, False, False)
    first = functools.partial(iteration, False, True)
    later = functools.partial(iteration, True, True)
    lax.fori_loop(0, FIRST_LATE, plain, 0)
    first(FIRST_LATE, 0)
    lax.fori_loop(FIRST_LATE + 1, ITERS, later, 0)

    n_anchor = anchors_ref.shape[0]
    order = lax.broadcasted_iota(jnp.int32, (n_anchor, step_pix), 0)
    wanted = jnp.zeros((n_anchor, step_pix), jnp.int32)
    for a in range(n_anchor):
        wanted = jnp.where(order == a, anchors_ref[a], wanted)
    wanted = wanted - pix * pixels - lo * half
    rows_half[...] = jnp.zeros_like(rows_half)

    def finish(j, carry):
        value = normal(gather(ITERS, j))
        slot = lo * chunks + j
        score[slot] = value
        send(score.at[slot], score.at[slot], sc_sem.at[j], (pix, mates[0])).start()
        positions = lax.broadcasted_iota(jnp.int32, (n_anchor, step_pix), 1)
        picks = jnp.where(positions == wanted - j * step_pix, 1.0, 0.0)
        rows_half[...] += dot(picks, value, NT, HIGH)
        return carry
    lax.fori_loop(0, chunks, finish, 0)
    pair_rows = send(rows_half, rows_half_in, rh_sem, (pix, mates[0]))
    pair_rows.start()
    pair_rows.wait()
    rows_out[...] = rows_half[...] + rows_half_in[...]

    def rows_copy(d, to):
        return send(rows_out, rows_in.at[d], rows_sem.at[d], (to, chan))
    all_pix(lambda d, to: rows_copy(d, to).start())
    rows_in[0] = rows_out[...]
    for j in range(chunks):
        slot = lo * chunks + j
        send(score.at[slot], score.at[slot], sc_sem.at[j], (pix, mates[0])).wait()
    for j in range(2 * chunks):
        part = slice(j * step_pix, (j + 1) * step_pix)
        scores_ref[:, part] = score[j]
        split_rows(pieces, score[j], part)
    all_pix(lambda d, to: rows_copy(d, to).wait())
    rows = jnp.sum(rows_in[...], axis=0)
    rows_pad[64 : 64 + n_anchor, :k_rows] = rows
    small = dot(rows_pad[64 : 64 + n_anchor, :], rows_pad[0:128, :], NT, HIGH)
    factor = inverse_factor(small)
    solved = dot(factor, rows_pad[64:192, :], precision=HIGH)
    both = dot(jnp.transpose(factor)[:n_anchor, :], solved, precision=HIGH)
    abund_ref[...] = split_dot(both, pieces[...])


def local(n_pix, spectra, start, anchors):
    pixels, ch = spectra.shape
    k = start.shape[0]
    na = anchors.shape[0]
    half = pixels // 2
    step = min(512, half)
    chunks = half // step
    n_hi = n_pix // GROUP
    vmem = pl.BlockSpec(memory_space=pltpu.VMEM)
    smem = pl.BlockSpec(memory_space=pltpu.SMEM)
    hbm = pl.BlockSpec(memory_space=pltpu.HBM)
    v = pltpu.VMEM
    sem = lambda *shape: pltpu.SemaphoreType.DMA(tuple(shape) + (2,))
    slabs = lambda count, kind: v((ITERS, count, 16, ch * k // (16 * GROUP)), kind)
    scratch = [
        v((pixels, ch), BF16), v((half, ch), BF16), v((k, ch), BF16), v((1, ch), F32),
        v((n_pix, 1, ch), F32), v((1, ch), F32), v((3, 1, ch), F32), v((2 * chunks, step), F32),
        v((3, 2 * chunks, step), F32), v((2 * chunks, 8, step), F32),
        v((chunks, step, 2 * ch), BF16), v((chunks, 2 * ch, step), BF16), v((k, 2 * ch), BF16),
        v((ITERS + 1, chunks, k, step), BF16), v((ITERS + 1, chunks, k, step), BF16),
        v((k, 2 * ch), F32), v((ITERS, k, ch), F32), v((ITERS, 2, k, ch), F32),
        v((ITERS, GROUP, k // GROUP, ch), F32), v((ITERS, n_hi, k // GROUP, ch), F32),
        v((ITERS, k, ch), F32), v((ITERS, k, ch), F32), v((3 * k, ch), F32),
        v((ITERS, k // 2, 2 * k), F32), v((ITERS, 3, k // 2, 2 * k), F32),
        v((2 * chunks, k, step), F32), v((na, k), F32), v((na, k), F32), v((na, k), F32),
        v((n_pix, na, k), F32), v((192, 128), F32),
        v((2 * k, 2 * ch), BF16), v((2 * k, step), BF16), v((k, 128), F32),
        v((2 * k, pixels), BF16),
        slabs(GROUP, BF16), slabs(GROUP, BF16), slabs(n_hi, F32), slabs(GROUP, BF16),
        slabs(GROUP, BF16), v((3 * k, ch), BF16),
        pltpu.SemaphoreType.DMA((2 * chunks,)), sem(chunks), sem(), sem(n_pix), sem(3), sem(3), sem(ITERS + 1, chunks), sem(ITERS),
        sem(ITERS, GROUP), sem(ITERS, n_hi), sem(ITERS, GROUP), sem(ITERS), sem(ITERS, 3),
        sem(chunks), sem(), sem(n_pix),
    ]
    return pl.pallas_call(
        functools.partial(kernel, n_pix),
        out_shape=(
            jax.ShapeDtypeStruct((k, pixels), F32),
            jax.ShapeDtypeStruct((na, pixels), F32),
        ),
        in_specs=[hbm, vmem, smem],
        out_specs=(vmem, vmem),
        scratch_shapes=scratch,
        compiler_params=pltpu.CompilerParams(
            collective_id=0, has_side_effects=True, vmem_limit_bytes=51 * 1024 * 1024
        ),
    )(spectra, start, anchors)


def solution(mesh):
    placed = (P("pix", "chan"), P(None, "chan"), P())
    return jax.shard_map(
        functools.partial(local, mesh.shape["pix"]),
        mesh=mesh,
        in_specs=placed,
        out_specs=(P(None, "pix"), P(None, "pix")),
        check_vma=False,
    )
```

```python
import functools

import jax
import jax.numpy as jnp
from jax import lax
from jax.experimental import pallas as pl
from jax.experimental.pallas import tpu as pltpu
from jax.sharding import PartitionSpec as P

ITERS = 5
FIRST_LATE = 2
GROUP = 8
MESH = pl.DeviceIdType.MESH
HIGH = lax.Precision.HIGHEST
F32 = jnp.float32
BF16 = jnp.bfloat16
NT = (((1,), (1,)), ((), ()))


def dot(a, b, dims=(((1,), (0,)), ((), ())), precision=None):
    return lax.dot_general(a, b, dims, precision=precision, preferred_element_type=F32)


def inverse_factor(gram):
    n = gram.shape[0]
    rows = lax.broadcasted_iota(jnp.int32, (n, 128), 0)
    lanes = lax.broadcasted_iota(jnp.int32, (n, 128), 1)
    full = jnp.where(lanes < 64, jnp.where(lanes == rows, 1.0, 0.0), gram)
    sub = lax.broadcasted_iota(jnp.int32, (8, 128), 0)
    count = n // 8
    blocks = [full[8 * i : 8 * i + 8, :] for i in range(count)]
    done = []
    for home in range(count):
        spread = [
            [jnp.broadcast_to(block[:, at : at + 1], (8, 128))
             for at in range(64 + 8 * home, 72 + 8 * home)]
            for block in blocks
        ]
        pivots = jnp.ones((8, 128), F32)
        for r in range(8):
            inverse = 1.0 / spread[0][r][r : r + 1, :]
            pivots = jnp.where(sub == r, spread[0][r], pivots)
            line = blocks[0][r : r + 1, :] * inverse
            later = {c: spread[0][c][r : r + 1, :] * inverse for c in range(r + 1, 8)}
            for i in range(len(blocks)):
                ratio = spread[i][r]
                if i == 0:
                    ratio = jnp.where(sub > r, ratio, 0.0)
                for c, value in later.items():
                    spread[i][c] = spread[i][c] - ratio * value
                blocks[i] = blocks[i] - ratio * line
        done.append(blocks[0] * lax.rsqrt(pivots))
        blocks = blocks[1:]
    return jnp.where(lanes < 64, jnp.concatenate(done, axis=0), 0.0)


def split_rows(ref, value, lanes):
    top = value.astype(BF16)
    n = value.shape[0]
    ref[:n, lanes] = top
    ref[n:, lanes] = (value - top.astype(F32)).astype(BF16)


def split_dot(left, pair):
    top = left.astype(BF16)
    low = (left - top.astype(F32)).astype(BF16)
    twice = (top.astype(F32) + pltpu.roll(top.astype(F32), 64, 1)).astype(BF16)
    n = left.shape[0]
    out = dot(jnp.concatenate([twice, low], axis=0), pair)
    return out[:n] + out[n:]


def kernel(
    n_pix, s_hbm, start_ref, anchors_ref, scores_ref, abund_ref,
    s_ref, other_s, start_in, col_out, col_in, col_mine, col_chan, row_out, row_in, row_sum,
    w, wt, load, x_out, x_in, acc, half_in, keep, rs_in, hi_in, ag, back_in, padded,
    gram_out, gram_in, score, rows_half, rows_half_in, rows_out, rows_in, rows_pad,
    halves, shares_split, factor_ref, pieces,
    keep16, rs16, hi16, ag16, back16_in, pad16, in_sem, s_sem, st_sem, col_sem, cc_sem, row_sem, x_sem, half_sem, rs_sem, hi_sem, ag_sem,
    bk_sem, gram_sem, sc_sem, rh_sem, rows_sem,
):
    pix = lax.axis_index("pix")
    chan = lax.axis_index("chan")
    lo, hi = lax.rem(chan, 2), lax.div(chan, 2)
    mates = [hi * 2 + 1 - lo, (1 - hi) * 2 + lo, (1 - hi) * 2 + 1 - lo]
    low = lax.rem(pix, GROUP)
    base = pix - low
    n_hi = n_pix // GROUP
    k_rows, ch = start_ref.shape
    pixels = s_ref.shape[0]
    half = pixels // 2
    step_pix = x_out.shape[-1]
    chunks = half // step_pix

    def send(src, dst, sems, device):
        return pltpu.make_async_remote_copy(
            src_ref=src, dst_ref=dst, send_sem=sems.at[0], recv_sem=sems.at[1],
            device_id=device, device_id_type=MESH,
        )

    def all_pix(f):
        def body(d, carry):
            f(d, lax.rem(pix + d, n_pix))
            return carry
        lax.fori_loop(1, n_pix, body, 0)

    loads = []
    for j in range(2 * chunks):
        part = pl.ds(j * step_pix, step_pix)
        loads.append(pltpu.make_async_copy(s_hbm.at[part], s_ref.at[part], in_sem.at[j]))
        loads[-1].start()

    barrier = pltpu.get_barrier_semaphore()
    for mate in mates:
        pl.semaphore_signal(barrier, inc=1, device_id=(pix, mate), device_id_type=MESH)
    all_pix(lambda d, to: pl.semaphore_signal(
        barrier, inc=1, device_id=(to, chan), device_id_type=MESH))
    pl.semaphore_wait(barrier, 3 + n_pix - 1)

    def swap_copy(j):
        away = pl.multiple_of(((1 - lo) * chunks + j) * step_pix, step_pix)
        return send(
            s_hbm.at[pl.ds(away, step_pix)],
            other_s.at[pl.ds(pl.multiple_of(j * step_pix, step_pix), step_pix)],
            s_sem.at[j], (pix, mates[0]))
    swap_start = send(start_ref, start_in, st_sem, (pix, mates[0]))
    swap_start.start()
    for j in range(chunks):
        swap_copy(j).start()

    total_col = jnp.zeros((8, ch), F32)
    for j in range(2 * chunks):
        loads[j].wait()
        block = s_ref[j * step_pix : (j + 1) * step_pix, :].astype(F32)
        total_col += jnp.sum(block.reshape(step_pix // 8, 8, ch), axis=0)
    col_out[...] = jnp.sum(total_col, axis=0, keepdims=True)

    def col_copy(d, to):
        return send(col_out, col_in.at[d], col_sem.at[d], (to, chan))
    all_pix(lambda d, to: col_copy(d, to).start())

    ones = jnp.ones((ch, 128), BF16)
    diagonal = lax.broadcasted_iota(jnp.int32, (128, 128), 0) == (
        lax.broadcasted_iota(jnp.int32, (128, 128), 1))
    for j in range(2 * chunks):
        sums = dot(s_ref[j * step_pix : (j + 1) * step_pix, :], ones)
        for b in range(step_pix // 128):
            square = jnp.where(diagonal, sums[b * 128 : (b + 1) * 128, :], 0.0)
            row_out[j : j + 1, b * 128 : (b + 1) * 128] = jnp.sum(
                square, axis=0, keepdims=True)
    row_copies = [
        send(row_out, row_in.at[m], row_sem.at[m], (pix, mates[m])) for m in range(3)
    ]
    for copy in row_copies:
        copy.start()

    col_in[0] = col_out[...]
    all_pix(lambda d, to: col_copy(d, to).wait())
    col_mine[...] = jnp.sum(col_in[...], axis=0)
    col_copies = [
        send(col_mine, col_chan.at[m], cc_sem.at[m], (pix, mates[m])) for m in range(3)
    ]
    for copy in col_copies:
        copy.start()
    for copy in row_copies:
        copy.wait()
    sums = (row_out[...] + row_in[0]) + (row_in[1] + row_in[2])
    for j in range(2 * chunks):
        row_sum[j] = jnp.broadcast_to(sums[j : j + 1, :], (8, step_pix))
    for copy in col_copies:
        copy.wait()
    cols = (col_mine[...] + col_chan[0]) + (col_chan[1] + col_chan[2])
    inv_total = 1.0 / jnp.sum(cols, axis=1, keepdims=True)
    shares = [col_mine[...] * inv_total, col_chan[0] * inv_total]
    share_roots = [lax.rsqrt(share) for share in shares]

    tiles = step_pix // 128

    swap_start.wait()
    load[:, :ch] = start_ref[...]
    load[:, ch:] = start_in[...]
    padded[...] = jnp.zeros_like(padded)
    pad16[...] = jnp.zeros_like(pad16)
    rows_pad[...] = jnp.zeros_like(rows_pad)

    def x_copy(t, j):
        return send(x_out.at[t, j], x_in.at[t, j], x_sem.at[t, j], (pix, mates[1]))

    def project_chunk(t, j):
        x_out[t, j] = dot(load[...], wt[j]).astype(BF16)
        x_copy(t, j).start()

    def project(t):
        def body(j, carry):
            project_chunk(t, j)
            return carry
        lax.fori_loop(0, chunks, body, 0)

    def gather(t, j):
        x_copy(t, j).wait()
        return x_out[t, j].astype(F32) + x_in[t, j].astype(F32)

    def normal(value):
        split_rows(shares_split, value, slice(0, step_pix))
        return split_dot(factor_ref[...], shares_split[...])

    def weigh(j, q):
        i = j * tiles + q
        first = pl.multiple_of(q * 128, 128)
        line = row_sum[lo * chunks + j, 0:1, pl.ds(first, 128)]
        wide = jnp.transpose(jnp.broadcast_to(line, (128, 128)))
        wide_root = lax.rsqrt(wide)
        mine = s_ref[pl.ds(pl.multiple_of(lo * half + i * 128, 128), 128), :]
        theirs = other_s[pl.ds(pl.multiple_of(i * 128, 128), 128), :]
        for side, counts in enumerate((mine, theirs)):
            for g in range(ch // 128):
                lanes = slice(g * 128, (g + 1) * 128)
                expect = wide * shares[side][:, lanes]
                root = wide_root * share_roots[side][:, lanes]
                value = counts[:, lanes].astype(F32)
                weighted = ((value - expect) * root).astype(BF16)
                at = side * ch + g * 128
                w[j, pl.ds(first, 128), at : at + 128] = weighted
                wt[j, at : at + 128, pl.ds(first, 128)] = jnp.transpose(weighted)

    def opening(j, carry):
        swap_copy(j).wait()

        def tile(q, inner):
            weigh(j, q)
            return inner
        lax.fori_loop(0, tiles, tile, 0)
        project_chunk(0, j)
        return carry
    lax.fori_loop(0, chunks, opening, 0)

    per = k_rows // GROUP

    def iteration(late, defer, t, carry):
        acc[...] = jnp.zeros_like(acc)

        def body(j, carry):
            value = gather(t, j)
            if late:
                value = normal(value)
            acc[...] += dot(value.astype(BF16), w[j])
            return carry
        lax.fori_loop(0, chunks, body, 0)

        keep[t, 0] = acc[:, ch:]
        copy = send(keep.at[t, 0], half_in.at[t], half_sem.at[t], (pix, mates[0]))
        copy.start()
        copy.wait()
        if defer:
            narrow(t)
        else:
            wide_sums(t)
        return carry

    def partner(d):
        return lax.rem(low + d, GROUP)

    def across_groups(t, slab, buffer):
        if n_hi == 1:
            return slab
        buffer[t, 0] = slab
        across = [
            send(buffer.at[t, 0], buffer.at[t, e], hi_sem.at[t, e],
                 (lax.rem(pix + e * GROUP, n_pix), chan))
            for e in range(1, n_hi)
        ]
        for copy in across:
            copy.start()
        for copy in across:
            copy.wait()
        place = lax.div(pix, GROUP)
        slab = buffer[t, lax.rem(n_hi + place, n_hi)]
        for e in range(1, n_hi):
            slab = slab + buffer[t, lax.rem(n_hi + place - e, n_hi)]
        return slab

    def gram_copies(t):
        return [
            send(gram_out.at[t], gram_in.at[t, m], gram_sem.at[t, m], (pix, mates[m]))
            for m in range(3)
        ]

    def factor_of(t):
        for copy in gram_copies(t):
            copy.wait()
        gram = (gram_out[t] + gram_in[t, 0]) + (gram_in[t, 1] + gram_in[t, 2])
        return inverse_factor(
            jnp.concatenate([pltpu.roll(gram, 64, 1), gram], axis=0))

    slab_lanes = ch * k_rows // (16 * GROUP)
    per_line = ch // slab_lanes

    def slab_at(i):
        return 16 * (i // per_line), (i % per_line) * slab_lanes

    def narrow(t):
        for i in range(GROUP):
            r, c = slab_at(i)
            part = acc[r : r + 16, c : c + slab_lanes]
            part = part + half_in[t, r : r + 16, c : c + slab_lanes]
            keep16[t, i] = part.astype(BF16)
        spread = [
            send(keep16.at[t, partner(d)], rs16.at[t, d], rs_sem.at[t, d],
                 (base + partner(d), chan))
            for d in range(1, GROUP)
        ]
        for copy in spread:
            copy.start()
        slab = keep16[t, low].astype(F32)
        for d, copy in enumerate(spread, 1):
            copy.wait()
            slab = slab + rs16[t, d].astype(F32)
        slab = across_groups(t, slab, hi16)
        ag16[t, low] = slab.astype(BF16)
        collect = [
            send(ag16.at[t, low], ag16.at[t, low], ag_sem.at[t, d], (base + partner(d), chan))
            for d in range(1, GROUP)
        ]
        for copy in collect:
            copy.start()
        for copy in collect:
            copy.wait()
        twin = send(ag16.at[t], back16_in.at[t], bk_sem.at[t], (pix, mates[0]))
        twin.start()
        for i in range(GROUP):
            r, c = slab_at(i)
            load[r : r + 16, c : c + slab_lanes] = ag16[t, i]
            pad16[k_rows + r : k_rows + r + 16, c : c + slab_lanes] = ag16[t, i]
        gram_out[t] = dot(load[: k_rows // 2, :ch], pad16[k_rows:, :], NT) + dot(
            load[k_rows // 2 :, :ch], pad16[: 2 * k_rows, :], NT)
        for copy in gram_copies(t):
            copy.start()
        twin.wait()
        for i in range(GROUP):
            r, c = slab_at(i)
            load[r : r + 16, ch + c : ch + c + slab_lanes] = back16_in[t, i]
        project(t + 1)
        factor_ref[...] = factor_of(t)

    def wide_sums(t):
        keep[t, 1] = acc[:, :ch] + half_in[t]
        spread = [
            send(
                keep.at[t, 1, pl.ds(pl.multiple_of(partner(d) * per, per), per)],
                rs_in.at[t, d], rs_sem.at[t, d], (base + partner(d), chan))
            for d in range(1, GROUP)
        ]
        for copy in spread:
            copy.start()
        slab = keep[t, 1, pl.ds(pl.multiple_of(low * per, per), per), :]
        for d, copy in enumerate(spread, 1):
            copy.wait()
            slab = slab + rs_in[t, d]
        slab = across_groups(t, slab, hi_in)
        mine = pl.ds(pl.multiple_of(low * per, per), per)
        ag[t, mine] = slab
        collect = [
            send(ag.at[t, mine], ag.at[t, mine], ag_sem.at[t, d], (base + partner(d), chan))
            for d in range(1, GROUP)
        ]
        for copy in collect:
            copy.start()
        for copy in collect:
            copy.wait()
        twin = send(ag.at[t], back_in.at[t], bk_sem.at[t], (pix, mates[0]))
        twin.start()
        back = ag[t]
        padded[k_rows : 2 * k_rows, :] = back
        gram_out[t] = dot(back[: k_rows // 2], padded[k_rows:, :], NT, HIGH) + dot(
            back[k_rows // 2 :], padded[: 2 * k_rows, :], NT, HIGH)
        for copy in gram_copies(t):
            copy.start()
        split_rows(halves, back, slice(0, ch))
        factor = factor_of(t)
        twin.wait()
        split_rows(halves, back_in[t], slice(ch, 2 * ch))
        load[...] = split_dot(factor, halves[...]).astype(BF16)
        project(t + 1)

    plain = functools.partial(iteration, False, False)
    first = functools.partial(iteration, False, True)
    later = functools.partial(iteration, True, True)
    lax.fori_loop(0, FIRST_LATE, plain, 0)
    first(FIRST_LATE, 0)
    lax.fori_loop(FIRST_LATE + 1, ITERS, later, 0)

    n_anchor = anchors_ref.shape[0]
    order = lax.broadcasted_iota(jnp.int32, (n_anchor, step_pix), 0)
    wanted = jnp.zeros((n_anchor, step_pix), jnp.int32)
    for a in range(n_anchor):
        wanted = jnp.where(order == a, anchors_ref[a], wanted)
    wanted = wanted - pix * pixels - lo * half
    rows_half[...] = jnp.zeros_like(rows_half)

    def finish(j, carry):
        value = normal(gather(ITERS, j))
        slot = lo * chunks + j
        score[slot] = value
        send(score.at[slot], score.at[slot], sc_sem.at[j], (pix, mates[0])).start()
        positions = lax.broadcasted_iota(jnp.int32, (n_anchor, step_pix), 1)
        picks = jnp.where(positions == wanted - j * step_pix, 1.0, 0.0).astype(BF16)
        top = value.astype(BF16)
        rest = (value - top.astype(F32)).astype(BF16)
        rows_half[...] += dot(picks, top, NT) + dot(picks, rest, NT)
        return carry
    lax.fori_loop(0, chunks, finish, 0)
    pair_rows = send(rows_half, rows_half_in, rh_sem, (pix, mates[0]))
    pair_rows.start()
    pair_rows.wait()
    rows_out[...] = rows_half[...] + rows_half_in[...]

    def rows_copy(d, to):
        return send(rows_out, rows_in.at[d], rows_sem.at[d], (to, chan))
    all_pix(lambda d, to: rows_copy(d, to).start())
    rows_in[0] = rows_out[...]
    for j in range(chunks):
        slot = lo * chunks + j
        send(score.at[slot], score.at[slot], sc_sem.at[j], (pix, mates[0])).wait()
    for j in range(2 * chunks):
        part = slice(j * step_pix, (j + 1) * step_pix)
        scores_ref[:, part] = score[j]
        split_rows(pieces, score[j], part)
    all_pix(lambda d, to: rows_copy(d, to).wait())
    rows = jnp.sum(rows_in[...], axis=0)
    rows_pad[64 : 64 + n_anchor, :k_rows] = rows
    small = dot(rows_pad[64 : 64 + n_anchor, :], rows_pad[0:128, :], NT, HIGH)
    factor = inverse_factor(small)
    solved = dot(factor, rows_pad[64:192, :], precision=HIGH)
    both = dot(jnp.transpose(factor)[:n_anchor, :], solved, precision=HIGH)
    abund_ref[...] = split_dot(both, pieces[...])


def local(n_pix, spectra, start, anchors):
    pixels, ch = spectra.shape
    k = start.shape[0]
    na = anchors.shape[0]
    half = pixels // 2
    step = min(512, half)
    chunks = half // step
    n_hi = n_pix // GROUP
    vmem = pl.BlockSpec(memory_space=pltpu.VMEM)
    smem = pl.BlockSpec(memory_space=pltpu.SMEM)
    hbm = pl.BlockSpec(memory_space=pltpu.HBM)
    v = pltpu.VMEM
    sem = lambda *shape: pltpu.SemaphoreType.DMA(tuple(shape) + (2,))
    slabs = lambda count, kind: v((ITERS, count, 16, ch * k // (16 * GROUP)), kind)
    scratch = [
        v((pixels, ch), BF16), v((half, ch), BF16), v((k, ch), BF16), v((1, ch), F32),
        v((n_pix, 1, ch), F32), v((1, ch), F32), v((3, 1, ch), F32), v((2 * chunks, step), F32),
        v((3, 2 * chunks, step), F32), v((2 * chunks, 8, step), F32),
        v((chunks, step, 2 * ch), BF16), v((chunks, 2 * ch, step), BF16), v((k, 2 * ch), BF16),
        v((ITERS + 1, chunks, k, step), BF16), v((ITERS + 1, chunks, k, step), BF16),
        v((k, 2 * ch), F32), v((ITERS, k, ch), F32), v((ITERS, 2, k, ch), F32),
        v((ITERS, GROUP, k // GROUP, ch), F32), v((ITERS, n_hi, k // GROUP, ch), F32),
        v((ITERS, k, ch), F32), v((ITERS, k, ch), F32), v((3 * k, ch), F32),
        v((ITERS, k // 2, 2 * k), F32), v((ITERS, 3, k // 2, 2 * k), F32),
        v((2 * chunks, k, step), F32), v((na, k), F32), v((na, k), F32), v((na, k), F32),
        v((n_pix, na, k), F32), v((192, 128), F32),
        v((2 * k, 2 * ch), BF16), v((2 * k, step), BF16), v((k, 128), F32),
        v((2 * k, pixels), BF16),
        slabs(GROUP, BF16), slabs(GROUP, BF16), slabs(n_hi, F32), slabs(GROUP, BF16),
        slabs(GROUP, BF16), v((3 * k, ch), BF16),
        pltpu.SemaphoreType.DMA((2 * chunks,)), sem(chunks), sem(), sem(n_pix), sem(3), sem(3), sem(ITERS + 1, chunks), sem(ITERS),
        sem(ITERS, GROUP), sem(ITERS, n_hi), sem(ITERS, GROUP), sem(ITERS), sem(ITERS, 3),
        sem(chunks), sem(), sem(n_pix),
    ]
    return pl.pallas_call(
        functools.partial(kernel, n_pix),
        out_shape=(
            jax.ShapeDtypeStruct((k, pixels), F32),
            jax.ShapeDtypeStruct((na, pixels), F32),
        ),
        in_specs=[hbm, vmem, smem],
        out_specs=(vmem, vmem),
        scratch_shapes=scratch,
        compiler_params=pltpu.CompilerParams(
            collective_id=0, has_side_effects=True, vmem_limit_bytes=51 * 1024 * 1024
        ),
    )(spectra, start, anchors)


def solution(mesh):
    placed = (P("pix", "chan"), P(None, "chan"), P())
    return jax.shard_map(
        functools.partial(local, mesh.shape["pix"]),
        mesh=mesh,
        in_specs=placed,
        out_specs=(P(None, "pix"), P(None, "pix")),
        check_vma=False,
    )
```
